256 devices in a mesh: group: 8 (over z_hi, x), shard: 32 (over y, z_lo, core).
Axes of the slice: x: 4, y: 4, z: 8 (z_hi: 2, z_lo: 4; z = z_hi * 4 + z_lo), core: 2. Of those that a mesh axis runs over, the one named last changes fastest.
Arguments:
- top_input: bfloat16 [32768, 3456], P(('group', 'shard')), may hold values from -6 to 6
- pre_act: bfloat16 [32768, 512], P(('group', 'shard')), may hold values from -6 to 6
- grad_hidden: bfloat16 [32768, 512], P(('group', 'shard')), may hold values from -6 to 6
- top_weight: bfloat16 [3456, 512], replicated, may hold values from -0.109375 to 0.109375
- core_first: bfloat16 [1024, 256], replicated, may hold values from -1 to 1
- core_mid: bfloat16 [1024, 2048], replicated, may hold values from -1 to 1
- core_last: bfloat16 [1024, 256], replicated, may hold values from -1 to 1
- bag_ids: int32 [8, 32, 4096], P('group', 'shard'), may hold values from 0 to 3327, never falling along the last dimension, each value on 1 to 8 neighbouring positions
- lookup_order: int32 [8, 32, 4096], P('group', 'shard'), may hold values from 0 to 4095, each once within a row
- hot_rows: int32 [8, 32, 3072], P('group', 'shard'), may hold values from 0 to 2047
- cold_digits: int32 [8, 32, 3, 1024], P('group', 'shard'), may hold values from 0 to 1023, as said below
Outputs:
- hot_grad: float32 [8, 65536, 128], P('group', 'shard')
- dense_grad: bfloat16 [32768, 128], P(('group', 'shard'))
- weight_grad: float32 [3456, 512], P('shard', 'group')
- first_grad: float32 [1024, 256], P('shard', 'group')
- mid_grad: float32 [1024, 2048], P('shard', 'group')
- last_grad: float32 [1024, 256], P('shard', 'group')
The draws below stay inside these ranges and needn't reach their ends.
Inputs may be any that keep to these rules, and one draw needn't show every extreme that they name: `bag_ids`: each device's lookups come in bag order; every one of its 3328 bags has 1 to 8 lookups. `lookup_order`: a permutation of each device's lookups: the first 3072 are hot, exactly 96 to each owner along shard in owner order, the rest cold. `cold_digits`: the j-th cold lookup of a device has its second digit in the block of 32 values numbered j // 32; first and third digits unconstrained.
All inputs are finite; a program needn't handle non-finite values.
Results may differ from the reference program's by a relative error of at most 0.0049.
Values may be sent and summed in bfloat16 or wider, within the bound.
A program may use at most 128 MiB of HBM per device.

```python
import math
import jax
import jax.numpy as jnp
import numpy as np
from jax import lax

E = 128
TABLES = 26
TOPW = 512
RANK = 32
NDIG = 1024
E1 = 8
E2 = 2
MOST = 8
B_DEV = 128
ROWS_DEV = 2048
E3 = 8
D_IN = 3456
LOOK = 4096
COLD_N = 1024
HOT_N = 3072
CAP = 96
GROUPS = 8
SHARDS = 32
HOT_ROWS = 65536
B_TOTAL = 32768


def draw_cold_digits(key, part):
    key = jax.random.fold_in(key, 11)
    key_one, key_two, key_three = jax.random.split(key, 3)
    shape = (GROUPS, SHARDS, COLD_N)
    block = NDIG // SHARDS
    per_owner = COLD_N // SHARDS
    first = jax.random.randint(key_one, shape, 0, NDIG)
    third = jax.random.randint(key_three, shape, 0, NDIG)
    owners = (jnp.arange(COLD_N, dtype=jnp.int32) // per_owner)[None, None, :]
    second = owners * block + jax.random.randint(key_two, shape, 0, block)
    return jnp.stack([first, second, third], axis=2).astype(jnp.int32)


def touch_ends(drawn, rng, least, high):
    dims = drawn.shape
    place = [jax.random.randint(jax.random.fold_in(rng, axis), (), 0, dims[axis]) for axis in range(len(dims))]
    drawn = drawn.at[tuple(place)].set(least)
    longest = dims.index(max(dims))
    place[longest] = (place[longest] + 1) % dims[longest]
    return drawn.at[tuple(place)].set(high)


def block_levels(rng, extent, cuts, low, top_value):
    loudness, own = 1.0, jax.random.fold_in(rng, 6)
    for dim, blocks in cuts:
        heights = jnp.exp(jax.random.uniform(jax.random.fold_in(own, dim), (blocks,), jnp.float32, low / len(cuts), top_value / len(cuts)))
        loudness = loudness * jnp.repeat(heights, extent[dim] // blocks).reshape([-1 if axis == dim else 1 for axis in range(len(extent))])
    return loudness


def cumulative_ranks(amount, skew):
    weights = [(1 << 20) // math.isqrt(standing ** skew) + 1 for standing in range(1, amount + 1)]
    deviation = 1 + sum(weights) // (1 << 30)
    return np.cumsum(np.array([max(1, weight // deviation) for weight in weights]))


def ranked(key, dims, count, lean):
    listing = cumulative_ranks(count, lean)
    pick = jax.random.randint(jax.random.fold_in(key, 1), dims, 0, int(listing[count - 1]))
    grade = jnp.searchsorted(jnp.asarray(listing, jnp.int32), pick, side="right")
    return jax.random.permutation(jax.random.fold_in(key, 2), count)[grade].astype(jnp.int32)


def split_up(number_of, total, bound, slope):
    loads = [(1 << 20) // math.isqrt(grade ** slope) + 1 for grade in range(2, number_of + 1)]
    spare, given = total - bound - (number_of - 1), [1] * (number_of - 1)
    while spare > 0:
        candidates = [i for i in range(number_of - 1) if given[i] < bound]
        pool, budget = sum([loads[i] for i in candidates]), spare
        for i in candidates:
            extra = min(bound - given[i], max(1, budget * loads[i] // pool), spare)
            given[i] = given[i] + extra
            spare = spare - extra
    return np.array([bound] + given)


def uneven(key, number_of, total, most, skew):
    if number_of == 2:
        one = jax.random.randint(key, (), max(1, total - most), min(most, total - 1) + 1)
        return jnp.stack([one, total - one])
    sizes = jnp.asarray(split_up(number_of, total, most, skew), jnp.int32)
    pairs = (number_of - 1) // 2
    source_of, taker = sizes[1:1 + 2 * pairs:2], sizes[2:2 + 2 * pairs:2]
    margin = jnp.minimum(source_of - 1, most - taker)
    passed = jax.random.randint(jax.random.fold_in(key, 1), (pairs,), 0, 1 << 20) % (margin + 1)
    sizes = sizes.at[1:1 + 2 * pairs:2].set(source_of - passed).at[2:2 + 2 * pairs:2].set(taker + passed)
    return sizes[jax.random.permutation(jax.random.fold_in(key, 2), number_of)]


def noise(key, extent, spread, reach, cuts=(), held_as=jnp.bfloat16):
    gain = block_levels(key, extent, cuts, -0.22, 0.18) if cuts else 1.0
    result = jax.random.normal(key, extent, jnp.float32) * spread * gain
    return jnp.minimum(jnp.maximum(result, -reach), reach).astype(held_as)


def setup_inputs(seed: int = 0) -> dict:
    key_of = jax.random.split(jax.random.key(seed), 12)
    return {
        "top_input": noise(key_of[0], (B_TOTAL, D_IN), 1.0, 6.0, ((0, 256),)),
        "pre_act": noise(key_of[1], (B_TOTAL, TOPW), 1.0, 6.0, ((0, 256),)),
        "grad_hidden": noise(key_of[2], (B_TOTAL, TOPW), 1.0, 6.0, ((0, 256),)),
        "top_weight": noise(key_of[3], (D_IN, TOPW), D_IN ** -0.5, 0.109375),
        "core_first": noise(key_of[4], (NDIG, E1 * RANK), 0.15, 1.0),
        "core_mid": noise(key_of[5], (NDIG, RANK * E2 * RANK), 0.15, 1.0),
        "core_last": noise(key_of[6], (NDIG, RANK * E3), 0.15, 1.0),
        "bag_ids": jax.vmap(lambda own: jnp.searchsorted(jnp.cumsum(uneven(own, B_DEV * TABLES, LOOK, MOST, 0)), jnp.arange(LOOK), side="right"))(jax.random.split(key_of[7], GROUPS * SHARDS)).reshape((GROUPS, SHARDS, LOOK)).astype(jnp.int32),
        "lookup_order": jax.vmap(lambda own: jax.random.permutation(own, LOOK))(jax.random.split(key_of[8], GROUPS * SHARDS)).reshape((GROUPS, SHARDS, LOOK)).astype(jnp.int32),
        "hot_rows": touch_ends(ranked(key_of[9], (GROUPS, SHARDS, HOT_N), ROWS_DEV, 2), jax.random.fold_in(key_of[9], 3), 0, ROWS_DEV - 1).astype(jnp.int32),
        "cold_digits": draw_cold_digits(jax.random.fold_in(key_of[11], 71), 0),
    }


def core_terms(grad, first, mid, last):
    high = lax.Precision.HIGHEST
    prod_p = jnp.einsum('cia,cajb->cijb', first, mid, precision=high)
    prod_q = jnp.einsum('cajb,cbk->cajk', mid, last, precision=high)
    prod_h = jnp.einsum('cia,cijk->cajk', first, grad, precision=high)
    term_first = jnp.einsum('cijk,cajk->cia', grad, prod_q, precision=high).astype(jnp.bfloat16)
    term_last = jnp.einsum('cijb,cijk->cbk', prod_p, grad, precision=high).astype(jnp.bfloat16)
    term_mid = jnp.einsum('cajk,cbk->cajb', prod_h, last, precision=high).astype(jnp.bfloat16)
    return term_first, term_mid, term_last


def reference(top_input, pre_act, grad_hidden, top_weight, core_first, core_mid, core_last, bag_ids, lookup_order, hot_rows, cold_digits):
    devices_all = GROUPS * SHARDS
    inputs = top_input.reshape(devices_all, B_DEV, D_IN)
    pres = pre_act.reshape(devices_all, B_DEV, TOPW)
    hiddens = grad_hidden.reshape(devices_all, B_DEV, TOPW)
    bags_all = bag_ids.reshape(devices_all, LOOK)
    orders = lookup_order.reshape(devices_all, LOOK)
    rows_all = hot_rows.reshape(devices_all, HOT_N)
    digits_all = cold_digits.reshape(devices_all, 3, COLD_N)
    owner = (jnp.arange(HOT_N, dtype=jnp.int32) // CAP).astype(jnp.int32)

    def step(carry, item):
        hot_acc, weight_acc, first_acc, mid_acc, last_acc = carry
        dev, inp, pre, hid, bags, order, rows, digits = item
        group_idx = (dev // SHARDS).astype(jnp.int32)
        pre_grad = jnp.where(pre > 0, hid, jnp.zeros_like(hid))
        weight_acc = weight_acc + jnp.dot(inp.T, pre_grad, preferred_element_type=jnp.float32)
        input_grad = jnp.dot(pre_grad, top_weight.T, preferred_element_type=jnp.float32)
        dense = input_grad[:, :E].astype(jnp.bfloat16)
        pooled = input_grad[:, E:].astype(jnp.bfloat16).reshape(B_DEV * TABLES, E)
        hot_bag = bags[order[:HOT_N]]
        sent = pooled[hot_bag].astype(jnp.float32)
        target = (group_idx * HOT_ROWS + owner * ROWS_DEV + rows).astype(jnp.int32)
        hot_acc = hot_acc.at[target].add(sent)
        cold_bag = bags[order[HOT_N:]]
        grad = pooled[cold_bag].astype(jnp.float32).reshape(COLD_N, E1, E2, E3)
        first = core_first[digits[0]].astype(jnp.float32).reshape(COLD_N, E1, RANK)
        mid = core_mid[digits[1]].astype(jnp.float32).reshape(COLD_N, RANK, E2, RANK)
        last = core_last[digits[2]].astype(jnp.float32).reshape(COLD_N, RANK, E3)
        term_first, term_mid, term_last = core_terms(grad, first, mid, last)
        term_first, term_mid, term_last = lax.optimization_barrier((term_first, term_mid, term_last))
        first_acc = first_acc + jax.ops.segment_sum(term_first.reshape(COLD_N, -1).astype(jnp.float32), digits[0], num_segments=NDIG)
        mid_acc = mid_acc + jax.ops.segment_sum(term_mid.reshape(COLD_N, -1).astype(jnp.float32), digits[1], num_segments=NDIG)
        last_acc = last_acc + jax.ops.segment_sum(term_last.reshape(COLD_N, -1).astype(jnp.float32), digits[2], num_segments=NDIG)
        return (hot_acc, weight_acc, first_acc, mid_acc, last_acc), dense

    start = (jnp.zeros((GROUPS * HOT_ROWS, E), jnp.float32), jnp.zeros((D_IN, TOPW), jnp.float32),
             jnp.zeros((NDIG, E1 * RANK), jnp.float32), jnp.zeros((NDIG, RANK * E2 * RANK), jnp.float32),
             jnp.zeros((NDIG, RANK * E3), jnp.float32))
    items = (jnp.arange(devices_all, dtype=jnp.int32), inputs, pres, hiddens, bags_all, orders, rows_all, digits_all)
    final, denses = lax.scan(step, start, items)
    hot_acc, weight_acc, first_acc, mid_acc, last_acc = final
    return (hot_acc.reshape(GROUPS, HOT_ROWS, E), denses.reshape(B_TOTAL, E), weight_acc, first_acc, mid_acc, last_acc)
```

```python
import functools

import jax
import jax.numpy as jnp
from jax import lax
from jax.experimental import pallas as pl
from jax.experimental.pallas import tpu as pltpu
from jax.sharding import PartitionSpec as P

F32 = jnp.float32
BF16 = jnp.bfloat16
I32 = jnp.int32

E = 128
RANK = 32
E1 = 8
E2 = 2
E3 = 8
HOT_N = 3072
SHARDS = 32
GROUPS = 8
PER_HOT = 96
PER_COLD = 32
BLOCK_W = 108
PAD_W = 112
ROWS = PAD_W + 32
MESH = pl.DeviceIdType.MESH


def iota(shape, dim):
    return lax.broadcasted_iota(I32, shape, dim)


def dot(a, b):
    return jnp.dot(a, b, preferred_element_type=F32)


def dot_nt(a, b):
    return lax.dot_general(a, b, (((1,), (1,)), ((), ())), preferred_element_type=F32)


def zero_one(mask):
    return jnp.where(mask, 1.0, 0.0).astype(BF16)


def kernel(
    act_ref, hid_ref, tw_ref, x_ref, rowmap, order, meta_ref, first_ref, last_ref, midq_ref, midl_ref,
    dense_ref, hot_ref, wout_ref, fout_ref, lout_ref, mout_ref,
    pooled, stage, send_c, send_h, recv_c, recv_h, recv_m,
    xt, xt_recv, pre2, w_own, ring,
    first_t, last_t, onehot, a_t, c_t, q_t, he, ce, qs, tnat, terms, mid_acc, mid_send, mid_recv,
    fl_own, fl_send, fl_recv, fx, fx_recv,
    ybuf, y_recv, zbuf, z_recv, h_send, h_recv,
    core_s, core_r, a_s, a_r, ring_s, ring_r, f_s, f_r, y_s, y_r, z_s, z_r, h_s, h_r, m_s, m_r,
):
    g = lax.axis_index("group")
    s = lax.axis_index("shard")
    xx = lax.rem(g, 4)
    zh = g // 4
    core = lax.rem(s, 2)
    zl = lax.rem(s // 2, 4)
    yy = s // 8

    def shard_at(y, z, c):
        return y * 8 + z * 2 + c

    def remote(src, dst, send_sem, recv_sem, to):
        return pltpu.make_async_remote_copy(
            src_ref=src, dst_ref=dst, send_sem=send_sem, recv_sem=recv_sem, device_id=to, device_id_type=MESH
        )

    partner = (g, shard_at(yy, zl, 1 - core))

    barrier = pltpu.get_barrier_semaphore()

    def greet_shard(k, carry):
        pl.semaphore_signal(barrier, inc=1, device_id=(g, lax.rem(s + k, SHARDS)), device_id_type=MESH)
        return carry

    def greet_group(k, carry):
        pl.semaphore_signal(barrier, inc=1, device_id=(lax.rem(g + k, GROUPS), s), device_id_type=MESH)
        return carry

    lax.fori_loop(1, SHARDS, greet_shard, 0)
    lax.fori_loop(1, GROUPS, greet_group, 0)

    pre = jnp.where(act_ref[...].astype(F32) > 0, hid_ref[...].astype(F32), 0.0).astype(BF16)
    col = iota((512, 512), 1)
    source = (col // 64 % 2) * 256 + (col // 128) * 64 + col % 64
    pre2[0:128, :] = dot(pre, zero_one(iota((512, 512), 0) == source)).astype(BF16)

    for shard in range(SHARDS):
        lo = shard * BLOCK_W // 128 * 128
        off = shard * BLOCK_W - lo
        width = 128 if off + BLOCK_W <= 128 else 256
        pick = zero_one(iota((PAD_W, width), 1) == iota((PAD_W, width), 0) + off)
        xt[shard % 2, shard // 2] = dot_nt(pick, x_ref[:, lo : lo + width]).astype(BF16)

    pl.semaphore_wait(barrier, SHARDS - 1 + GROUPS - 1)

    send_pre = remote(pre2.at[0:128], pre2.at[128:256], core_s.at[0], core_r.at[0], partner)
    send_pre.start()
    send_xt = remote(xt.at[1 - core], xt_recv, core_s.at[1], core_r.at[1], partner)
    send_xt.start()

    dense_ref[...] = dot_nt(pre, tw_ref[0:128, :]).astype(BF16)

    def pool(i, carry):
        rows = tw_ref[pl.ds(pl.multiple_of(128 + i * 256, 128), 256), :]
        part = dot_nt(pre, rows).astype(BF16).astype(F32)
        pooled[pl.ds(pl.multiple_of(i * 256, 128), 128), :] = part[:, 0:128]
        pooled[pl.ds(pl.multiple_of(i * 256 + 128, 128), 128), :] = part[:, 128:256]
        return carry

    lax.fori_loop(0, 13, pool, 0)

    send_pre.wait()
    send_xt.wait()
    pre_both = pre2[...]

    def product(j, carry):
        both = jnp.concatenate([xt[core, j], xt_recv[j]], axis=1)
        part = dot(both, pre_both).astype(BF16)
        for k in range(4):
            w_own[k, j] = part[:, k * 128 : (k + 1) * 128]
        return carry

    lax.fori_loop(0, 16, product, 0)

    right = (zh * 4 + lax.rem(xx + 1, 4), s)
    left = (zh * 4 + lax.rem(xx + 3, 4), s)

    def ring_copy(way, step):
        to = right if way == 0 else left
        if step == 0:
            chunk = lax.rem(xx + 3, 4) if way == 0 else lax.rem(xx + 1, 4)
            src = w_own.at[chunk, pl.ds(way * 8, 8)]
        else:
            src = ring.at[way, step - 1]
        return remote(src, ring.at[way, step], ring_s.at[way, step], ring_r.at[way, step], to)

    def ring_add(way, step):
        chunk = lax.rem(xx + 2 - step, 4) if way == 0 else lax.rem(xx + 2 + step, 4)

        def add(j, carry):
            total = ring[way, step, j].astype(F32) + w_own[chunk, way * 8 + j].astype(F32)
            ring[way, step, j] = total.astype(BF16)
            return carry

        lax.fori_loop(0, 8, add, 0)

    def ring_next(step):
        for way in range(2):
            ring_copy(way, step - 1).wait()
            ring_add(way, step - 1)
            ring_copy(way, step).start()

    for way in range(2):
        ring_copy(way, 0).start()

    def gather(base, count):
        for j in range(count):
            r = rowmap[order[base + j]]
            stage[pl.ds(j, 1), :] = pooled[pl.ds(r, 1), :]
        return stage[0:count, :].astype(BF16)

    def cold_to(k, carry):
        o = lax.rem(s + k, SHARDS)
        send_c[k] = gather(HOT_N + o * PER_COLD, PER_COLD)
        remote(send_c.at[k], recv_c.at[s], a_s.at[0], a_r.at[0], (g, o)).start()
        remote(meta_ref.at[o], recv_m.at[s], a_s.at[1], a_r.at[1], (g, o)).start()
        return carry

    def hot_to(k, carry):
        o = lax.rem(s + k, SHARDS)
        send_h[k] = gather(o * PER_HOT, PER_HOT)
        remote(send_h.at[k], recv_h.at[s], a_s.at[2], a_r.at[2], (g, o)).start()
        return carry

    lax.fori_loop(1, SHARDS, cold_to, 0)
    send_c[0] = gather(HOT_N + s * PER_COLD, PER_COLD)
    pltpu.make_async_copy(send_c.at[0], recv_c.at[s], a_r.at[0]).start()
    pltpu.make_async_copy(meta_ref.at[s], recv_m.at[s], a_r.at[1]).start()
    lax.fori_loop(1, SHARDS, hot_to, 0)
    send_h[0] = gather(s * PER_HOT, PER_HOT)
    pltpu.make_async_copy(send_h.at[0], recv_h.at[s], a_r.at[2]).start()

    ring_next(1)

    eye = zero_one(iota((256, 256), 0) == iota((256, 256), 1))
    first_t[...] = dot_nt(eye, first_ref[...]).astype(BF16)
    turn_row = iota((256, 256), 0)
    turn = zero_one(iota((256, 256), 1) == (turn_row % 32) * 8 + turn_row // 32)
    last_t[...] = dot_nt(turn, last_ref[...]).astype(BF16)
    mid_acc[...] = jnp.zeros_like(mid_acc)

    pltpu.make_async_copy(recv_c, recv_c, a_r.at[0]).wait()
    pltpu.make_async_copy(recv_m, recv_m, a_r.at[1]).wait()

    def cold_tile(t, carry):
        lanes = pl.ds(pl.multiple_of(t * 128, 128), 128)
        lanes_last = pl.ds(pl.multiple_of(1024 + t * 128, 128), 128)

        def digits(row):
            four = recv_m[pl.ds(4 * t, 4), row : row + 1, :]
            return four[0] + four[1] + four[2] + four[3]

        one, two, three = digits(3), digits(4), digits(5)
        for k in range(4):
            rows = slice(k * 256, (k + 1) * 256)
            place = iota((256, 128), 0) + k * 256
            onehot[rows, lanes] = zero_one(place == one)
            onehot[rows, lanes_last] = zero_one(place == three)
        a_t[...] = dot(first_t[...], onehot[:, lanes])
        c_t[...] = dot(last_t[...], onehot[:, lanes_last])
        q_t[...] = recv_c[pl.ds(4 * t, 4)].reshape(128, 128).astype(F32).T
        low, high = two % 4, two // 4
        low2 = jnp.concatenate([low, low], axis=1)
        high2 = jnp.concatenate([high, high], axis=1)
        for pair in range(4):
            cols = slice(pair * 256, (pair + 1) * 256)
            for e2 in range(2):
                halves = []
                for e3 in (2 * pair, 2 * pair + 1):
                    total = None
                    for e1 in range(8):
                        q_row = e1 * 16 + e2 * 8 + e3
                        term = a_t[e1 * 32 : (e1 + 1) * 32, :] * q_t[q_row : q_row + 1, :]
                        total = term if total is None else total + term
                    halves.append(total)
                h = jnp.concatenate(halves, axis=1)
                for k in range(4):
                    he[k * 64 + e2 * 32 : k * 64 + e2 * 32 + 32, cols] = jnp.where(low2 == k, h, 0.0).astype(BF16)
            c = jnp.concatenate(
                [c_t[e3 * 32 : (e3 + 1) * 32, :] for e3 in (2 * pair, 2 * pair + 1)], axis=1
            )
            for k in range(8):
                ce[k * 32 : (k + 1) * 32, cols] = jnp.where(high2 == k, c, 0.0).astype(BF16)
            q_all = dot(midq_ref[...], ce[:, cols])
            total = jnp.zeros((64, 256), F32)
            for k in range(4):
                total = total + jnp.where(low2 == k, q_all[k * 64 : (k + 1) * 64, :], 0.0)
            qs[:, cols] = total
            l_all = dot(midl_ref[...], he[:, cols])
            total = jnp.zeros((32, 256), F32)
            for k in range(8):
                total = total + jnp.where(high2 == k, l_all[k * 32 : (k + 1) * 32, :], 0.0)
            total = total.astype(BF16)
            tnat[256 + pair * 64 : 256 + pair * 64 + 32, lanes] = total[:, 0:128]
            tnat[256 + pair * 64 + 32 : 256 + pair * 64 + 64, lanes] = total[:, 128:256]
        mid_acc[...] += dot_nt(he[...], ce[...])
        for e1 in range(8):
            total = None
            for e2 in range(2):
                for e3 in range(8):
                    q_row = e1 * 16 + e2 * 8 + e3
                    term = qs[e2 * 32 : (e2 + 1) * 32, e3 * 128 : (e3 + 1) * 128] * q_t[q_row : q_row + 1, :]
                    total = term if total is None else total + term
            tnat[e1 * 32 : (e1 + 1) * 32, lanes] = total.astype(BF16)
        return carry

    lax.fori_loop(0, 4, cold_tile, 0)
    ring_next(2)
    lax.fori_loop(4, 8, cold_tile, 0)

    row = iota((256, 256), 0)
    source = (row // 2 % 4) * 64 + (row % 2) * 32 + ((row // 32 % 2) * 4 + row // 64) * 4 + row // 8 % 4
    moved = dot(zero_one(iota((256, 256), 1) == source), mid_acc[...].astype(BF16)).astype(BF16)
    for k in range(8):
        mid_send[k] = moved[k * 32 : (k + 1) * 32, :]

    def mid_copy(d):
        to = lax.rem(g + d, GROUPS)
        src = mid_send.at[lax.rem(to, 4) * 2 + to // 4]
        return remote(src, mid_recv.at[d - 1], m_s.at[d - 1], m_r.at[d - 1], (to, s))

    for d in range(1, GROUPS):
        mid_copy(d).start()

    row = iota((512, 256), 0)
    owner = (row // 64 % 2) * 4 + row // 128
    is_first = row % 64 < 32
    j = row % 32
    lane = iota((512, 256), 1)
    place_first = zero_one(is_first & (lane == owner * 32 + j))
    place_last = zero_one((row % 64 >= 32) & (lane == (j % 8) * 32 + owner * 4 + j // 8))
    for k in range(4):
        cols = slice(k * 256, (k + 1) * 256)
        terms[:, cols] = dot(place_first, tnat[0:256, cols]).astype(BF16)
        terms[:, 1024 + k * 256 : 1024 + (k + 1) * 256] = dot(place_last, tnat[256:512, cols]).astype(BF16)

    def by_digit(k, carry):
        part = dot_nt(onehot[pl.ds(pl.multiple_of(k * 256, 256), 256), :], terms[...])
        for i in range(4):
            for c in range(2):
                fl_own[c, 4 * k + i] = part[(2 * i + c) * 32 : (2 * i + c + 1) * 32, :]
        return carry

    lax.fori_loop(0, 4, by_digit, 0)

    def fl_round(j, carry):
        fl_send[j] = fl_own[1 - core, j].astype(BF16)
        return carry

    lax.fori_loop(0, 16, fl_round, 0)
    fl_copy = remote(fl_send, fl_recv, core_s.at[2], core_r.at[2], partner)
    fl_copy.start()

    pltpu.make_async_copy(recv_h, recv_h, a_r.at[2]).wait()
    hot_ref[...] = jnp.zeros_like(hot_ref)

    def hot_part(i, carry):
        ids = []
        for half in range(2):
            four = recv_m[pl.ds(8 * i + 4 * half, 4), :, :]
            four = four[0] + four[1] + four[2] + four[3]
            ids += [four[k : k + 1, :] for k in range(3)]
        values = recv_h[pl.ds(8 * i, 8)].reshape(768, 128).astype(F32)
        low = jnp.concatenate(ids, axis=1) % 512
        pick = zero_one(iota((512, 768), 0) == low)
        column = jnp.concatenate(
            [jnp.broadcast_to((r // 512).astype(F32), (128, 128)).T for r in ids], axis=0
        )
        for k in range(4):
            part = jnp.where(column == float(k), values, 0.0).astype(BF16)
            hot_ref[k * 512 : (k + 1) * 512, :] += dot(pick, part)
        return carry

    lax.fori_loop(0, 4, hot_part, 0)

    fl_copy.wait()

    def fl_pair(j, carry):
        total = (fl_own[core, j] + fl_recv[j].astype(F32)).astype(BF16)
        for k in range(4):
            fx[k, j] = total[:, k * 128 : (k + 1) * 128]
        return carry

    lax.fori_loop(0, 16, fl_pair, 0)

    def fl_x(d):
        to = lax.rem(xx + d, 4)
        return remote(fx.at[to], fx_recv.at[d - 1], f_s.at[d - 1], f_r.at[d - 1], (zh * 4 + to, s))

    for d in range(1, 4):
        fl_x(d).start()

    for way in range(2):
        ring_copy(way, 2).wait()

        def last_add(j, carry):
            total = ring[way, 2, j].astype(F32) + w_own[xx, way * 8 + j].astype(F32)
            ybuf[way * 8 + j, 0:PAD_W, :] = total.astype(BF16)
            return carry

        lax.fori_loop(0, 8, last_add, 0)

    for d in range(1, 4):
        fl_x(d).wait()

    def fl_x_add(j, carry):
        total = fx[xx, j].astype(F32)
        for d in range(3):
            total = total + fx_recv[d, j].astype(F32)
        ybuf[j, PAD_W:ROWS, :] = total.astype(BF16)
        return carry

    lax.fori_loop(0, 16, fl_x_add, 0)

    def y_copy(d):
        to = lax.rem(yy + d, 4)
        src = ybuf.at[pl.ds(4 * to, 4)]
        return remote(src, y_recv.at[d - 1], y_s.at[d - 1], y_r.at[d - 1], (g, shard_at(to, zl, core)))

    for d in range(1, 4):
        y_copy(d).start()
    for d in range(1, 4):
        y_copy(d).wait()
    for j in range(4):
        total = ybuf[4 * yy + j].astype(F32)
        for d in range(3):
            total = total + y_recv[d, j].astype(F32)
        zbuf[j] = total.astype(BF16)

    def z_copy(d):
        to = lax.rem(zl + d, 4)
        return remote(zbuf.at[to], z_recv.at[d - 1], z_s.at[d - 1], z_r.at[d - 1], (g, shard_at(yy, to, core)))

    for d in range(1, 4):
        z_copy(d).start()
    for d in range(1, 4):
        z_copy(d).wait()
    total = zbuf[zl].astype(F32)
    for d in range(3):
        total = total + z_recv[d].astype(F32)
    h_send[...] = total.astype(BF16)

    far = remote(h_send, h_recv, h_s.at[0], h_r.at[0], (lax.rem(g + 4, 8), s))
    far.start()

    for d in range(1, GROUPS):
        mid_copy(d).wait()
    mid_total = mid_send[xx * 2 + zh].astype(F32)
    for d in range(GROUPS - 1):
        mid_total = mid_total + mid_recv[d].astype(F32)
    mout_ref[...] = mid_total

    far.wait()
    total = total + h_recv[...].astype(F32)
    total = jnp.where(zh == 0, total, pltpu.roll(total, 64, 1))
    wout_ref[...] = total[0:BLOCK_W, 0:64]
    fout_ref[...] = total[PAD_W:ROWS, 0:32]
    lout_ref[...] = total[PAD_W:ROWS, 32:64]

    sent = send_c.at[pl.ds(1, SHARDS - 1)]
    pltpu.make_async_copy(sent, sent, a_s.at[0]).wait()
    sent = recv_m.at[pl.ds(1, SHARDS - 1)]
    pltpu.make_async_copy(sent, sent, a_s.at[1]).wait()
    sent = send_h.at[pl.ds(1, SHARDS - 1)]
    pltpu.make_async_copy(sent, sent, a_s.at[2]).wait()


def body(
    top_input,
    pre_act,
    grad_hidden,
    top_weight,
    core_first,
    core_mid,
    core_last,
    bag_ids,
    lookup_order,
    hot_rows,
    cold_digits,
):
    s = lax.axis_index("shard")
    bags = bag_ids[0, 0]
    rowmap = bags % 26 * 128 + bags // 26
    order = lookup_order[0, 0]
    mine = (jnp.arange(4) == s % 4).astype(I32)
    hot = hot_rows[0, 0].reshape(SHARDS, 1, PER_HOT) * mine[None, :, None]
    digits = cold_digits[0, 0].reshape(3, SHARDS, 1, PER_COLD)
    digits = digits - (jnp.arange(3) == 1).astype(I32)[:, None, None, None] * (
        jnp.arange(SHARDS, dtype=I32)[None, :, None, None] * 32
    )
    digits = (digits * mine[None, None, :, None]).reshape(3, SHARDS, 128)
    meta = jnp.concatenate(
        [hot.reshape(SHARDS, 3, 128), digits.transpose(1, 0, 2), jnp.zeros((SHARDS, 2, 128), I32)], axis=1
    )
    block = lax.dynamic_slice_in_dim(core_mid, s * 32, 32, 0).reshape(8, 4, RANK, E2, RANK)
    midq = block.transpose(1, 3, 2, 0, 4).reshape(256, 256)
    midl = block.transpose(0, 4, 1, 3, 2).reshape(256, 256)

    vmem = pl.BlockSpec(memory_space=pltpu.VMEM)
    smem = pl.BlockSpec(memory_space=pltpu.SMEM)

    def buf(*shape, dtype=BF16):
        return pltpu.VMEM(shape, dtype)

    dma = pltpu.SemaphoreType.DMA
    outs = pl.pallas_call(
        kernel,
        out_shape=(
            jax.ShapeDtypeStruct((128, 128), BF16),
            jax.ShapeDtypeStruct((2048, 128), F32),
            jax.ShapeDtypeStruct((BLOCK_W, 64), F32),
            jax.ShapeDtypeStruct((32, 32), F32),
            jax.ShapeDtypeStruct((32, 32), F32),
            jax.ShapeDtypeStruct((32, 256), F32),
        ),
        in_specs=[vmem, vmem, vmem, vmem, smem, smem, vmem, vmem, vmem, vmem, vmem],
        out_specs=(vmem,) * 6,
        scratch_shapes=[
            buf(26 * 128, 128, dtype=F32),
            buf(PER_HOT, 128, dtype=F32),
            buf(SHARDS, PER_COLD, 128),
            buf(SHARDS, PER_HOT, 128),
            buf(SHARDS, PER_COLD, 128),
            buf(SHARDS, PER_HOT, 128),
            buf(SHARDS, 8, 128, dtype=I32),
            buf(2, 16, PAD_W, 128),
            buf(16, PAD_W, 128),
            buf(256, 512),
            buf(4, 16, PAD_W, 128),
            buf(2, 3, 8, PAD_W, 128),
            buf(256, 1024),
            buf(256, 1024),
            buf(1024, 2048),
            buf(256, 128, dtype=F32),
            buf(256, 128, dtype=F32),
            buf(128, 128, dtype=F32),
            buf(256, 1024),
            buf(256, 1024),
            buf(64, 1024, dtype=F32),
            buf(512, 1024),
            buf(512, 2048),
            buf(256, 256, dtype=F32),
            buf(8, 32, 256),
            buf(7, 32, 256),
            buf(2, 16, 32, 512, dtype=F32),
            buf(16, 32, 512),
            buf(16, 32, 512),
            buf(4, 16, 32, 128),
            buf(3, 16, 32, 128),
            buf(16, ROWS, 128),
            buf(3, 4, ROWS, 128),
            buf(4, ROWS, 128),
            buf(3, ROWS, 128),
            buf(ROWS, 128),
            buf(ROWS, 128),
            dma((3,)),
            dma((3,)),
            dma((3,)),
            dma((3,)),
            dma((2, 3)),
            dma((2, 3)),
            dma((3,)),
            dma((3,)),
            dma((3,)),
            dma((3,)),
            dma((3,)),
            dma((3,)),
            dma((1,)),
            dma((1,)),
            dma((7,)),
            dma((7,)),
        ],
        compiler_params=pltpu.CompilerParams(
            collective_id=0, has_side_effects=True, vmem_limit_bytes=56 * 1024 * 1024
        ),
    )(
        pre_act,
        grad_hidden,
        top_weight,
        top_input,
        rowmap,
        order,
        meta,
        core_first,
        core_last,
        midq,
        midl,
    )
    dense_grad, hot_grad, weight_grad, first_grad, last_grad, mid = outs
    mid_grad = mid.reshape(4, 4, E2, 8, RANK).transpose(3, 1, 0, 2, 4).reshape(32, 256)
    return (hot_grad[None], dense_grad, weight_grad, first_grad, mid_grad, last_grad)


def solution(mesh):
    return jax.shard_map(
        body,
        mesh=mesh,
        in_specs=(
            P(("group", "shard"), None),
            P(("group", "shard"), None),
            P(("group", "shard"), None),
            P(),
            P(),
            P(),
            P(),
            P("group", "shard", None),
            P("group", "shard", None),
            P("group", "shard", None),
            P("group", "shard", None, None),
        ),
        out_specs=(
            P("group", "shard", None),
            P(("group", "shard"), None),
            P("shard", "group"),
            P("shard", "group"),
            P("shard", "group"),
            P("shard", "group"),
        ),
        check_vma=False,
    )
```

```python
import functools

import jax
import jax.numpy as jnp
from jax import lax
from jax.experimental import pallas as pl
from jax.experimental.pallas import tpu as pltpu
from jax.sharding import PartitionSpec as P

F32 = jnp.float32
BF16 = jnp.bfloat16
I32 = jnp.int32

E = 128
RANK = 32
E1 = 8
E2 = 2
E3 = 8
HOT_N = 3072
SHARDS = 32
GROUPS = 8
PER_HOT = 96
PER_COLD = 32
BLOCK_W = 108
PAD_W = 112
ROWS = PAD_W + 32
MESH = pl.DeviceIdType.MESH


def iota(shape, dim):
    return lax.broadcasted_iota(I32, shape, dim)


def dot(a, b):
    return jnp.dot(a, b, preferred_element_type=F32)


def dot_nt(a, b):
    return lax.dot_general(a, b, (((1,), (1,)), ((), ())), preferred_element_type=F32)


def zero_one(mask):
    return jnp.where(mask, 1.0, 0.0).astype(BF16)


def kernel(
    act_hbm, hid_hbm, tw_hbm, x_hbm, bags, order, hot_in, dig_in, first_hbm, last_hbm, midq_ref,
    dense_ref, hot_hbm, wout_ref, fout_ref, lout_ref, mout_ref,
    act_ref, hid_ref, tw_ref, x_ref, first_ref, last_ref, midl, hot,
    pooled, stage, meta, send_c, send_h, recv_c, recv_h, recv_m,
    xt, xt_recv, pre2, w_own, ring,
    first_t, last_t, onehot, a_t, c_t, q_t, he, ce, qs, tf, tl, mid_acc, mid_send, mid_recv,
    fl_own, fl_send, fl_recv, fx, fx_recv,
    wy, wy_recv, wz, wz_recv, fy, fy_recv, fz, fz_recv,
    load_s, core_s, core_r, a_s, a_r, ring_s, ring_r, f_s, f_r, wy_s, wy_r, wz_s, wz_r,
    fy_s, fy_r, fz_s, fz_r, m_s, m_r,
):
    g = lax.axis_index("group")
    s = lax.axis_index("shard")
    xx = lax.rem(g, 4)
    zh = g // 4
    core = lax.rem(s, 2)
    zl = lax.rem(s // 2, 4)
    yy = s // 8
    deep = zh * 4 + zl

    load_act = pltpu.make_async_copy(act_hbm, act_ref, load_s.at[0])
    load_hid = pltpu.make_async_copy(hid_hbm, hid_ref, load_s.at[1])
    load_x = pltpu.make_async_copy(x_hbm, x_ref, load_s.at[2])
    load_tw = pltpu.make_async_copy(tw_hbm, tw_ref, load_s.at[3])
    load_first = pltpu.make_async_copy(first_hbm, first_ref, load_s.at[4])
    load_last = pltpu.make_async_copy(last_hbm, last_ref, load_s.at[5])
    load_act.start()
    load_hid.start()
    load_x.start()
    load_tw.start()
    load_first.start()
    load_last.start()

    def shard_at(y, z, c):
        return y * 8 + z * 2 + c

    def remote(src, dst, send_sem, recv_sem, to):
        return pltpu.make_async_remote_copy(
            src_ref=src, dst_ref=dst, send_sem=send_sem, recv_sem=recv_sem, device_id=to, device_id_type=MESH
        )

    def along_z(d):
        to = lax.rem(deep + d, 8)
        return to, ((to // 4) * 4 + xx, shard_at(yy, lax.rem(to, 4), core))

    partner = (g, shard_at(yy, zl, 1 - core))

    barrier = pltpu.get_barrier_semaphore()

    def greet_shard(k, carry):
        pl.semaphore_signal(barrier, inc=1, device_id=(g, lax.rem(s + k, SHARDS)), device_id_type=MESH)
        return carry

    def greet_group(k, carry):
        pl.semaphore_signal(barrier, inc=1, device_id=(lax.rem(g + k, GROUPS), s), device_id_type=MESH)
        return carry

    def greet_far(k, carry):
        to = (lax.rem(g + 4, 8), shard_at(yy, lax.rem(zl + k, 4), core))
        pl.semaphore_signal(barrier, inc=1, device_id=to, device_id_type=MESH)
        return carry

    lax.fori_loop(1, SHARDS, greet_shard, 0)
    lax.fori_loop(1, GROUPS, greet_group, 0)
    lax.fori_loop(1, 4, greet_far, 0)

    meta[...] = jnp.zeros_like(meta)
    mine = lax.rem(s, 4)
    hots = jnp.concatenate([hot_in[pl.ds(c, 8, stride=3), :] for c in range(3)], axis=1)

    def place(values, width, i):
        lane = iota(values.shape, 1)
        kept = jnp.where((lane >= i * width) & (lane < (i + 1) * width), values, 0)
        out = kept
        for j in range(4):
            if j != i:
                out = jnp.where(mine == j, pltpu.roll(kept, (j - i) % 4 * width, 1), out)
        return out

    for i in range(4):
        out = place(hots, PER_HOT, i)
        for q in range(8):
            for c in range(3):
                meta[4 * q + i, c : c + 1, :] = out[q : q + 1, c * 128 : (c + 1) * 128]
    for r in range(3):
        digit = dig_in[0, 0, r : r + 1, :]
        if r == 1:
            digit = digit % 32
        digit = jnp.concatenate([digit[:, q * 128 : (q + 1) * 128] for q in range(8)], axis=0)
        for i in range(4):
            out = place(digit, PER_COLD, i)
            for q in range(8):
                meta[4 * q + i, 3 + r : 4 + r, :] = out[q : q + 1, :]

    load_act.wait()
    load_hid.wait()
    pre = jnp.where(act_ref[...].astype(F32) > 0, hid_ref[...].astype(F32), 0.0).astype(BF16)
    col = iota((512, 512), 1)
    source = (col // 64 % 2) * 256 + (col // 128) * 64 + col % 64
    pre2[0:128, :] = dot(pre, zero_one(iota((512, 512), 0) == source)).astype(BF16)

    load_x.wait()
    for shard in range(SHARDS):
        lo = shard * BLOCK_W // 128 * 128
        off = shard * BLOCK_W - lo
        width = 128 if off + BLOCK_W <= 128 else 256
        pick = zero_one(iota((PAD_W, width), 1) == iota((PAD_W, width), 0) + off)
        xt[shard % 2, shard // 2] = dot_nt(pick, x_ref[:, lo : lo + width]).astype(BF16)

    pl.semaphore_wait(barrier, SHARDS - 1 + GROUPS - 1 + 3)
    send_pre = remote(pre2.at[0:128], pre2.at[128:256], core_s.at[0], core_r.at[0], partner)
    send_pre.start()
    send_xt = remote(xt.at[1 - core], xt_recv, core_s.at[1], core_r.at[1], partner)
    send_xt.start()

    load_tw.wait()
    dense_ref[...] = dot_nt(pre, tw_ref[0:128, :]).astype(BF16)
    for i in range(13):
        part = dot_nt(pre, tw_ref[128 + i * 256 : 384 + i * 256, :]).astype(BF16).astype(F32)
        pooled[pl.ds(2 * i, 128, stride=26), :] = part[:, 0:128]
        pooled[pl.ds(2 * i + 1, 128, stride=26), :] = part[:, 128:256]

    def gather(base, count):
        for j in range(count):
            r = bags[0, 0, order[0, 0, base + j]]
            stage[pl.ds(j, 1), :] = pooled[pl.ds(r, 1), :]
        return stage[0:count, :].astype(BF16)

    def cold_to(k, carry):
        o = lax.rem(s + k, SHARDS)
        send_c[k] = gather(HOT_N + o * PER_COLD, PER_COLD)
        remote(send_c.at[k], recv_c.at[s], a_s.at[0], a_r.at[0], (g, o)).start()
        remote(meta.at[o], recv_m.at[s], a_s.at[1], a_r.at[1], (g, o)).start()
        return carry

    def hot_to(k, carry):
        o = lax.rem(s + k, SHARDS)
        send_h[k] = gather(o * PER_HOT, PER_HOT)
        remote(send_h.at[k], recv_h.at[s], a_s.at[2], a_r.at[2], (g, o)).start()
        return carry

    lax.fori_loop(1, SHARDS, cold_to, 0)
    send_c[0] = gather(HOT_N + s * PER_COLD, PER_COLD)
    pltpu.make_async_copy(send_c.at[0], recv_c.at[s], a_r.at[0]).start()
    pltpu.make_async_copy(meta.at[s], recv_m.at[s], a_r.at[1]).start()

    send_pre.wait()
    send_xt.wait()
    pre_both = pre2[...]
    for j in range(0, 16, 4):
        both = jnp.concatenate(
            [xt[core, j : j + 4].reshape(4 * PAD_W, 128), xt_recv[j : j + 4].reshape(4 * PAD_W, 128)], axis=1
        )
        part = dot(both, pre_both).astype(BF16)
        for k in range(4):
            w_own[k, j : j + 4] = part[:, k * 128 : (k + 1) * 128].reshape(4, PAD_W, 128)

    right = (zh * 4 + lax.rem(xx + 1, 4), s)
    left = (zh * 4 + lax.rem(xx + 3, 4), s)

    def ring_copy(way, step):
        to = right if way == 0 else left
        if step == 0:
            chunk = lax.rem(xx + 3, 4) if way == 0 else lax.rem(xx + 1, 4)
            src = w_own.at[chunk, pl.ds(way * 8, 8)]
        else:
            src = ring.at[way, step - 1]
        return remote(src, ring.at[way, step], ring_s.at[way, step], ring_r.at[way, step], to)

    def ring_add(way, step):
        chunk = lax.rem(xx + 2 - step, 4) if way == 0 else lax.rem(xx + 2 + step, 4)

        def add(j, carry):
            total = ring[way, step, j].astype(F32) + w_own[chunk, way * 8 + j].astype(F32)
            ring[way, step, j] = total.astype(BF16)
            return carry

        lax.fori_loop(0, 8, add, 0)

    def ring_next(step):
        for way in range(2):
            ring_copy(way, step - 1).wait()
            ring_add(way, step - 1)
            ring_copy(way, step).start()

    for way in range(2):
        ring_copy(way, 0).start()

    lax.fori_loop(1, SHARDS, hot_to, 0)
    send_h[0] = gather(s * PER_HOT, PER_HOT)
    pltpu.make_async_copy(send_h.at[0], recv_h.at[s], a_r.at[2]).start()

    load_first.wait()
    load_last.wait()
    eye = zero_one(iota((256, 256), 0) == iota((256, 256), 1))
    first_t[...] = dot_nt(eye, first_ref[...]).astype(BF16)
    turn_row = iota((256, 256), 0)
    turn = zero_one(iota((256, 256), 1) == (turn_row % 32) * 8 + turn_row // 32)
    last_t[...] = dot_nt(turn, last_ref[...]).astype(BF16)
    midl[...] = dot_nt(eye, midq_ref[...]).astype(BF16)
    mid_acc[...] = jnp.zeros_like(mid_acc)

    ring_next(1)

    pltpu.make_async_copy(recv_c, recv_c, a_r.at[0]).wait()
    pltpu.make_async_copy(recv_m, recv_m, a_r.at[1]).wait()

    def digits(t, row):
        four = recv_m[pl.ds(4 * t, 4), row : row + 1, :]
        return four[0] + four[1] + four[2] + four[3]

    def pick_cores(u, carry):
        lanes = pl.ds(pl.multiple_of(u * 256, 256), 256)
        for i, (table, out) in enumerate(((first_t, a_t), (last_t, c_t))):
            digit = jnp.concatenate([digits(2 * u, 3 + 2 * i), digits(2 * u + 1, 3 + 2 * i)], axis=1)
            for k in range(4):
                row = iota((256, 256), 0) + k * 256
                onehot[i, k * 256 : (k + 1) * 256, lanes] = zero_one(row == digit)
            part = dot(table[...], onehot[i, :, lanes])
            out[2 * u] = part[:, 0:128]
            out[2 * u + 1] = part[:, 128:256]
        return carry

    lax.fori_loop(0, 4, pick_cores, 0)

    def cold_tile(t, carry):
        lanes = pl.ds(pl.multiple_of(t * 128, 128), 128)
        two = digits(t, 4)
        q_t[...] = recv_c[pl.ds(4 * t, 4)].reshape(128, 128).astype(F32).T
        low = jnp.broadcast_to(jnp.concatenate([two % 4, two % 4], axis=1), (8, 256))
        high = jnp.broadcast_to(jnp.concatenate([two // 4, two // 4], axis=1), (8, 256))
        is_low = [low == k for k in range(4)]
        is_high = [high == k for k in range(8)]

        def packed(mask):
            half = jnp.where(mask, 1.0, 0.0)
            return jnp.concatenate([half, half], axis=0).astype(BF16)

        keep_low = [packed(m) for m in is_low]
        keep_high = [packed(m) for m in is_high]
        for pair in range(4):
            cols = slice(pair * 256, (pair + 1) * 256)
            for e2 in range(2):
                halves = []
                for e3 in (2 * pair, 2 * pair + 1):
                    total = None
                    for e1 in range(8):
                        q_row = e1 * 16 + e2 * 8 + e3
                        term = a_t[t, e1 * 32 : (e1 + 1) * 32, :] * q_t[q_row : q_row + 1, :]
                        total = term if total is None else total + term
                    halves.append(total)
                h = jnp.concatenate(halves, axis=1).astype(BF16).reshape(2, 16, 256)
                for k in range(4):
                    he[k * 64 + e2 * 32 : k * 64 + e2 * 32 + 32, cols] = (h * keep_low[k][None]).reshape(32, 256)
            c = jnp.concatenate(
                [c_t[t, e3 * 32 : (e3 + 1) * 32, :] for e3 in (2 * pair, 2 * pair + 1)], axis=1
            )
            c = c.astype(BF16).reshape(2, 16, 256)
            for k in range(8):
                ce[k * 32 : (k + 1) * 32, cols] = (c * keep_high[k][None]).reshape(32, 256)
            q_all = dot(midq_ref[...], ce[:, cols]).reshape(4, 8, 8, 256)
            total = q_all[0]
            for k in range(1, 4):
                total = jnp.where(is_low[k][None], q_all[k], total)
            qs[:, cols] = total.reshape(64, 256)
            l_all = dot(midl[...], he[:, cols]).reshape(8, 4, 8, 256)
            total = l_all[0]
            for k in range(1, 8):
                total = jnp.where(is_high[k][None], l_all[k], total)
            total = total.reshape(32, 256).astype(BF16)
            tl[pair * 64 : pair * 64 + 32, lanes] = total[:, 0:128]
            tl[pair * 64 + 32 : pair * 64 + 64, lanes] = total[:, 128:256]
        mid_acc[...] += dot_nt(he[...], ce[...])
        for e1 in range(8):
            total = None
            for e2 in range(2):
                for e3 in range(8):
                    q_row = e1 * 16 + e2 * 8 + e3
                    term = qs[e2 * 32 : (e2 + 1) * 32, e3 * 128 : (e3 + 1) * 128] * q_t[q_row : q_row + 1, :]
                    total = term if total is None else total + term
            row = (e1 % 4) * 64 + (e1 // 4) * 32
            tf[row : row + 32, lanes] = total.astype(BF16)
        return carry

    lax.fori_loop(0, 4, cold_tile, 0)
    ring_next(2)
    lax.fori_loop(4, 8, cold_tile, 0)

    row = iota((256, 256), 0)
    j = row % 32
    source = (j % 8) * 32 + ((row // 32 % 2) * 4 + row // 64) * 4 + j // 8
    tl[...] = dot(zero_one(iota((256, 256), 1) == source), tl[...]).astype(BF16)
    lane = iota((256, 128), 1)

    def by_digit(k, carry):
        rows = pl.ds(pl.multiple_of(k * 256, 256), 256)
        one = dot_nt(onehot[0, rows, :], tf[...])
        two = dot_nt(onehot[1, rows, :], tl[...])
        for i in range(4):
            a = one[:, i // 2 * 128 : i // 2 * 128 + 128]
            b = two[:, i // 2 * 128 : i // 2 * 128 + 128]
            if i % 2 == 0:
                part = jnp.where(lane < 64, a, pltpu.roll(b, 64, 1))
            else:
                part = jnp.where(lane < 64, pltpu.roll(a, 64, 1), b)
            for n in range(8):
                fl_own[n % 2, i, 4 * k + n // 2] = part[n * 32 : (n + 1) * 32, :]
        return carry

    lax.fori_loop(0, 4, by_digit, 0)

    def fl_round(j, carry):
        for i in range(4):
            fl_send[i, j] = fl_own[1 - core, i, j].astype(BF16)
        return carry

    lax.fori_loop(0, 16, fl_round, 0)
    fl_copy = remote(fl_send, fl_recv, core_s.at[2], core_r.at[2], partner)
    fl_copy.start()

    row = iota((256, 256), 0)
    source = (row % 4) * 64 + (row // 4 % 2) * 32 + ((row // 32 % 2) * 4 + row // 64) * 4 + row // 8 % 4
    moved = dot(zero_one(iota((256, 256), 1) == source), mid_acc[...].astype(BF16)).astype(BF16)
    for k in range(8):
        mid_send[k] = moved[k * 32 : (k + 1) * 32, :]

    def mid_copy(d):
        to = lax.rem(g + d, GROUPS)
        src = mid_send.at[lax.rem(to, 4) * 2 + to // 4]
        return remote(src, mid_recv.at[d - 1], m_s.at[d - 1], m_r.at[d - 1], (to, s))

    for d in range(1, GROUPS):
        mid_copy(d).start()

    for way in range(2):
        ring_copy(way, 2).wait()

        def last_add(j, carry):
            total = ring[way, 2, j].astype(F32) + w_own[xx, way * 8 + j].astype(F32)
            wy[way * 8 + j] = total.astype(BF16)
            return carry

        lax.fori_loop(0, 8, last_add, 0)

    def y_copy(buf, into, send_sem, recv_sem, d):
        to = lax.rem(yy + d, 4)
        src = buf.at[pl.ds(4 * to, 4)]
        return remote(src, into.at[d - 1], send_sem.at[d - 1], recv_sem.at[d - 1], (g, shard_at(to, zl, core)))

    for d in range(1, 4):
        y_copy(wy, wy_recv, wy_s, wy_r, d).start()

    fl_copy.wait()

    def fl_pair(j, carry):
        for i in range(4):
            fx[i, j] = (fl_own[core, i, j] + fl_recv[i, j].astype(F32)).astype(BF16)
        return carry

    lax.fori_loop(0, 16, fl_pair, 0)

    def fl_x(d):
        to = lax.rem(xx + d, 4)
        return remote(fx.at[to], fx_recv.at[d - 1], f_s.at[d - 1], f_r.at[d - 1], (zh * 4 + to, s))

    for d in range(1, 4):
        fl_x(d).start()

    pltpu.make_async_copy(recv_h, recv_h, a_r.at[2]).wait()
    hot[...] = jnp.zeros_like(hot)

    def hot_part(i, carry):
        ids = []
        for half in range(2):
            four = recv_m[pl.ds(8 * i + 4 * half, 4), :, :]
            four = four[0] + four[1] + four[2] + four[3]
            ids += [four[k : k + 1, :] for k in range(3)]
        values = recv_h[pl.ds(8 * i, 8)].reshape(768, 128).astype(F32)
        low = jnp.concatenate(ids, axis=1) % 512
        pick = zero_one(iota((512, 768), 0) == low)
        column = jnp.concatenate(
            [jnp.broadcast_to((r // 512).astype(F32), (128, 128)).T for r in ids], axis=0
        )
        for k in range(0, 4, 2):
            both = [jnp.where(column == float(k + n), values, 0.0).astype(BF16) for n in range(2)]
            part = dot(pick, jnp.concatenate(both, axis=1))
            hot[k * 512 : (k + 1) * 512, :] += part[:, 0:128]
            hot[(k + 1) * 512 : (k + 2) * 512, :] += part[:, 128:256]
        return carry

    lax.fori_loop(0, 4, hot_part, 0)
    save_hot = pltpu.make_async_copy(hot, hot_hbm, load_s.at[6])
    save_hot.start()

    for d in range(1, 4):
        fl_x(d).wait()

    def fl_x_add(j, carry):
        total = fx[xx, j].astype(F32)
        for d in range(3):
            total = total + fx_recv[d, j].astype(F32)
        fy[j] = total.astype(BF16)
        return carry

    lax.fori_loop(0, 16, fl_x_add, 0)
    for d in range(1, 4):
        y_copy(fy, fy_recv, fy_s, fy_r, d).start()

    for d in range(1, 4):
        y_copy(wy, wy_recv, wy_s, wy_r, d).wait()

    def halves(total, count, width):
        top, bottom = total[0:count], total[count : 2 * count]
        left_half = iota((count, 128), 1) % (2 * width) < width
        return (
            jnp.where(left_half, top, pltpu.roll(bottom, width, 1)),
            jnp.where(left_half, pltpu.roll(top, 128 - width, 1), bottom),
        )

    def z_copy(buf, into, send_sem, recv_sem, d):
        to, device = along_z(d)
        return remote(buf.at[to], into.at[d - 1], send_sem.at[d - 1], recv_sem.at[d - 1], device)

    for j in range(4):
        total = wy[4 * yy + j].astype(F32)
        for d in range(3):
            total = total + wy_recv[d, j].astype(F32)
        for k, half in enumerate(halves(total, 56, 64)):
            wz[4 * k + j] = jnp.concatenate([half, jnp.zeros((8, 128), F32)], axis=0).astype(BF16)
    for d in range(1, 8):
        z_copy(wz, wz_recv, wz_s, wz_r, d).start()

    for d in range(1, 4):
        y_copy(fy, fy_recv, fy_s, fy_r, d).wait()
    for j in range(4):
        total = fy[4 * yy + j].astype(F32)
        for d in range(3):
            total = total + fy_recv[d, j].astype(F32)
        for k, half in enumerate(halves(total, 16, 32)):
            fz[4 * k + j] = half.astype(BF16)
    for d in range(1, 8):
        z_copy(fz, fz_recv, fz_s, fz_r, d).start()

    for d in range(1, GROUPS):
        mid_copy(d).wait()
    total = mid_send[xx * 2 + zh].astype(F32)
    for d in range(GROUPS - 1):
        total = total + mid_recv[d].astype(F32)
    mout_ref[...] = total

    for d in range(1, 8):
        z_copy(wz, wz_recv, wz_s, wz_r, d).wait()
    total = wz[deep].astype(F32)
    for d in range(7):
        total = total + wz_recv[d].astype(F32)
    wout_ref[0:56, :] = total[0:56, 0:64]
    wout_ref[56:BLOCK_W, :] = pltpu.roll(total, 64, 1)[0 : BLOCK_W - 56, 0:64]

    for d in range(1, 8):
        z_copy(fz, fz_recv, fz_s, fz_r, d).wait()
    total = fz[deep].astype(F32)
    for d in range(7):
        total = total + fz_recv[d].astype(F32)
    fout_ref[0:16, :] = total[:, 0:32]
    fout_ref[16:32, :] = pltpu.roll(total, 96, 1)[:, 0:32]
    lout_ref[0:16, :] = pltpu.roll(total, 64, 1)[:, 0:32]
    lout_ref[16:32, :] = pltpu.roll(total, 32, 1)[:, 0:32]

    save_hot.wait()
    sent = send_c.at[pl.ds(1, SHARDS - 1)]
    pltpu.make_async_copy(sent, sent, a_s.at[0]).wait()
    sent = recv_m.at[pl.ds(1, SHARDS - 1)]
    pltpu.make_async_copy(sent, sent, a_s.at[1]).wait()
    sent = send_h.at[pl.ds(1, SHARDS - 1)]
    pltpu.make_async_copy(sent, sent, a_s.at[2]).wait()


def finish(dense, hot, weight, first, last, mid, dense_out, hot_out, weight_out, first_out, last_out, mid_out):
    dense_out[...] = dense[...]
    hot_out[...] = hot[...]
    weight_out[...] = weight[...]
    first_out[...] = first[...]
    last_out[...] = last[...]
    for m1 in range(8):
        parts = []
        for a in range(4):
            for e2 in range(2):
                row = a * 8 + e2 * 4
                parts.append(mid[row : row + 4, m1 * 32 : (m1 + 1) * 32])
        mid_out[m1 * 4 : (m1 + 1) * 4, :] = jnp.concatenate(parts, axis=1)


def body(
    top_input,
    pre_act,
    grad_hidden,
    top_weight,
    core_first,
    core_mid,
    core_last,
    bag_ids,
    lookup_order,
    hot_rows,
    cold_digits,
):
    s = lax.axis_index("shard")
    block = lax.dynamic_slice_in_dim(core_mid, s * 32, 32, 0).reshape(8, 4, RANK, E2, RANK)
    midq = block.transpose(1, 3, 2, 0, 4).reshape(256, 256)

    vmem = pl.BlockSpec(memory_space=pltpu.VMEM)
    smem = pl.BlockSpec(memory_space=pltpu.SMEM)
    hbm = pl.BlockSpec(memory_space=pl.ANY)

    def buf(*shape, dtype=BF16):
        return pltpu.VMEM(shape, dtype)

    dma = pltpu.SemaphoreType.DMA
    shapes = (
        jax.ShapeDtypeStruct((128, 128), BF16),
        jax.ShapeDtypeStruct((2048, 128), F32),
        jax.ShapeDtypeStruct((BLOCK_W, 64), F32),
        jax.ShapeDtypeStruct((32, 32), F32),
        jax.ShapeDtypeStruct((32, 32), F32),
        jax.ShapeDtypeStruct((32, 256), F32),
    )
    outs = pl.pallas_call(
        kernel,
        out_shape=shapes,
        in_specs=[hbm, hbm, hbm, hbm, smem, smem, vmem, vmem, hbm, hbm, vmem],
        out_specs=(vmem, hbm, vmem, vmem, vmem, vmem),
        scratch_shapes=[
            buf(128, 512),
            buf(128, 512),
            buf(3456, 512),
            buf(128, 3456),
            buf(1024, 256),
            buf(1024, 256),
            buf(256, 256),
            buf(2048, 128, dtype=F32),
            buf(26 * 128, 128, dtype=F32),
            buf(PER_HOT, 128, dtype=F32),
            buf(SHARDS, 8, 128, dtype=I32),
            buf(SHARDS, PER_COLD, 128),
            buf(SHARDS, PER_HOT, 128),
            buf(SHARDS, PER_COLD, 128),
            buf(SHARDS, PER_HOT, 128),
            buf(SHARDS, 8, 128, dtype=I32),
            buf(2, 16, PAD_W, 128),
            buf(16, PAD_W, 128),
            buf(256, 512),
            buf(4, 16, PAD_W, 128),
            buf(2, 3, 8, PAD_W, 128),
            buf(256, 1024),
            buf(256, 1024),
            buf(2, 1024, 1024),
            buf(8, 256, 128, dtype=F32),
            buf(8, 256, 128, dtype=F32),
            buf(128, 128, dtype=F32),
            buf(256, 1024),
            buf(256, 1024),
            buf(64, 1024, dtype=F32),
            buf(256, 1024),
            buf(256, 1024),
            buf(256, 256, dtype=F32),
            buf(8, 32, 256),
            buf(7, 32, 256),
            buf(2, 4, 16, 32, 128, dtype=F32),
            buf(4, 16, 32, 128),
            buf(4, 16, 32, 128),
            buf(4, 16, 32, 128),
            buf(3, 16, 32, 128),
            buf(16, PAD_W, 128),
            buf(3, 4, PAD_W, 128),
            buf(8, 64, 128),
            buf(7, 64, 128),
            buf(16, 32, 128),
            buf(3, 4, 32, 128),
            buf(8, 16, 128),
            buf(7, 16, 128),
            dma((7,)),
            dma((3,)),
            dma((3,)),
            dma((3,)),
            dma((3,)),
            dma((2, 3)),
            dma((2, 3)),
            dma((3,)),
            dma((3,)),
            dma((3,)),
            dma((3,)),
            dma((7,)),
            dma((7,)),
            dma((3,)),
            dma((3,)),
            dma((7,)),
            dma((7,)),
            dma((7,)),
            dma((7,)),
        ],
        compiler_params=pltpu.CompilerParams(
            collective_id=0, has_side_effects=True, vmem_limit_bytes=56 * 1024 * 1024
        ),
    )(
        pre_act,
        grad_hidden,
        top_weight,
        top_input,
        bag_ids,
        lookup_order,
        hot_rows.reshape(24, 128),
        cold_digits,
        core_first,
        core_last,
        midq,
    )
    dense_grad, hot_grad, weight_grad, first_grad, last_grad, mid_grad = pl.pallas_call(
        finish,
        out_shape=shapes,
        in_specs=[vmem] * 6,
        out_specs=(vmem,) * 6,
    )(*outs)
    return (hot_grad[None], dense_grad, weight_grad, first_grad, mid_grad, last_grad)


def solution(mesh):
    return jax.shard_map(
        body,
        mesh=mesh,
        in_specs=(
            P(("group", "shard"), None),
            P(("group", "shard"), None),
            P(("group", "shard"), None),
            P(),
            P(),
            P(),
            P(),
            P("group", "shard", None),
            P("group", "shard", None),
            P("group", "shard", None),
            P("group", "shard", None, None),
        ),
        out_specs=(
            P("group", "shard", None),
            P(("group", "shard"), None),
            P("shard", "group"),
            P("shard", "group"),
            P("shard", "group"),
            P("shard", "group"),
        ),
        check_vma=False,
    )
```

```python
import functools

import jax
import jax.numpy as jnp
from jax import lax
from jax.experimental import pallas as pl
from jax.experimental.pallas import tpu as pltpu
from jax.sharding import PartitionSpec as P

F32 = jnp.float32
BF16 = jnp.bfloat16
I32 = jnp.int32

E = 128
RANK = 32
E1 = 8
E2 = 2
E3 = 8
HOT_N = 3072
SHARDS = 32
GROUPS = 8
PER_HOT = 96
PER_COLD = 32
BLOCK_W = 108
PAD_W = 112
ROWS = PAD_W + 32
MESH = pl.DeviceIdType.MESH


def iota(shape, dim):
    return lax.broadcasted_iota(I32, shape, dim)


def dot(a, b):
    return jnp.dot(a, b, preferred_element_type=F32)


def dot_nt(a, b):
    return lax.dot_general(a, b, (((1,), (1,)), ((), ())), preferred_element_type=F32)


def zero_one(mask):
    return jnp.where(mask, 1.0, 0.0).astype(BF16)


def kernel(
    act_hbm, hid_hbm, tw_hbm, x_hbm, bags, order, hot_in, dig_in, first_hbm, last_hbm, mid_hbm,
    dense_ref, hot_hbm, wout_ref, fout_ref, lout_ref, mout_ref,
    act_ref, hid_ref, tw_ref, x_ref, first_ref, last_ref, mid_block, mid_turned, midq, midl, hot,
    pooled, stage, meta, send_c, send_h, recv_c, recv_h, recv_m,
    xt, xt_recv, pre2, w_own, ring,
    first_t, last_t, onehot, a_t, c_t, q_t, he, ce, qs, tf, tl, mid_acc, mid_send, mid_recv,
    fl_own, fl_send, fl_recv, fa, fa_recv, fb, fb_recv, fa2, fa2_recv, fb2, fb2_recv,
    wy, wy_recv, wz, wz_recv, fz, fz_recv,
    load_s, core_s, core_r, a_s, a_r, ring_s, ring_r, f_s, f_r, wy_s, wy_r, wz_s, wz_r,
    fz_s, fz_r, m_s, m_r,
):
    g = lax.axis_index("group")
    s = lax.axis_index("shard")
    xx = lax.rem(g, 4)
    zh = g // 4
    core = lax.rem(s, 2)
    zl = lax.rem(s // 2, 4)
    yy = s // 8
    deep = zh * 4 + zl

    load_act = pltpu.make_async_copy(act_hbm, act_ref, load_s.at[0])
    load_hid = pltpu.make_async_copy(hid_hbm, hid_ref, load_s.at[1])
    load_x = pltpu.make_async_copy(x_hbm, x_ref, load_s.at[2])
    load_tw = pltpu.make_async_copy(tw_hbm, tw_ref, load_s.at[3])
    load_first = pltpu.make_async_copy(first_hbm, first_ref, load_s.at[4])
    load_last = pltpu.make_async_copy(last_hbm, last_ref, load_s.at[5])
    load_mid = pltpu.make_async_copy(mid_hbm.at[pl.ds(pl.multiple_of(s * 32, 32), 32)], mid_block, load_s.at[7])
    load_act.start()
    load_hid.start()
    load_x.start()
    load_tw.start()
    load_first.start()
    load_last.start()
    load_mid.start()

    def shard_at(y, z, c):
        return y * 8 + z * 2 + c

    def remote(src, dst, send_sem, recv_sem, to):
        return pltpu.make_async_remote_copy(
            src_ref=src, dst_ref=dst, send_sem=send_sem, recv_sem=recv_sem, device_id=to, device_id_type=MESH
        )

    def along_z(d):
        to = lax.rem(deep + d, 8)
        return to, ((to // 4) * 4 + xx, shard_at(yy, lax.rem(to, 4), core))

    partner = (g, shard_at(yy, zl, 1 - core))

    barrier = pltpu.get_barrier_semaphore()

    def greet_shard(k, carry):
        pl.semaphore_signal(barrier, inc=1, device_id=(g, lax.rem(s + k, SHARDS)), device_id_type=MESH)
        return carry

    def greet_group(k, carry):
        pl.semaphore_signal(barrier, inc=1, device_id=(lax.rem(g + k, GROUPS), s), device_id_type=MESH)
        return carry

    def greet_far(k, carry):
        to = (lax.rem(g + 4, 8), shard_at(yy, lax.rem(zl + k, 4), core))
        pl.semaphore_signal(barrier, inc=1, device_id=to, device_id_type=MESH)
        return carry

    lax.fori_loop(1, SHARDS, greet_shard, 0)
    lax.fori_loop(1, GROUPS, greet_group, 0)
    lax.fori_loop(1, 4, greet_far, 0)

    turns = lax.rem(s, 4)

    def turned(values, width):
        out = values
        for n in range(1, 4):
            out = jnp.where(turns == n, pltpu.roll(values, (4 - n) * width, 1), out)
        return out

    def kept(values, width, i):
        low = lax.rem(i + 4 - turns, 4) * width
        lane = iota(values.shape, 1)
        return jnp.where((lane >= low) & (lane < low + width), values, 0)

    hots = turned(jnp.concatenate([hot_in[pl.ds(c, 8, stride=3), :] for c in range(3)], axis=1), PER_HOT)
    one_three = turned(dig_in[0:8, :] + dig_in[16:24, :] * 65536, PER_COLD)
    two = turned(dig_in[8:16, :] % 32 * 65536, PER_COLD)
    for i in range(4):
        hot_i = kept(hots, PER_HOT, i)
        rows = [hot_i[:, c * 128 : (c + 1) * 128] for c in range(3)] + [kept(one_three, PER_COLD, i)]
        rows[0] = rows[0] + kept(two, PER_COLD, i)
        for q in range(8):
            for c in range(4):
                meta[4 * q + i, c : c + 1, :] = rows[c][q : q + 1, :]

    load_act.wait()
    load_hid.wait()
    pre = jnp.where(act_ref[...].astype(F32) > 0, hid_ref[...].astype(F32), 0.0).astype(BF16)
    col = iota((512, 512), 1)
    source = (col // 64 % 2) * 256 + (col // 128) * 64 + col % 64
    pre2[0:128, :] = dot(pre, zero_one(iota((512, 512), 0) == source)).astype(BF16)

    load_x.wait()
    for shard in range(SHARDS):
        lo = shard * BLOCK_W // 128 * 128
        off = shard * BLOCK_W - lo
        width = 128 if off + BLOCK_W <= 128 else 256
        pick = zero_one(iota((PAD_W, width), 1) == iota((PAD_W, width), 0) + off)
        xt[shard % 2, shard // 2] = dot_nt(pick, x_ref[:, lo : lo + width]).astype(BF16)

    load_tw.wait()
    dense_ref[...] = dot_nt(pre, tw_ref[0:128, :]).astype(BF16)
    for i in range(13):
        part = dot_nt(pre, tw_ref[128 + i * 256 : 384 + i * 256, :]).astype(BF16).astype(F32)
        pooled[pl.ds(2 * i, 128, stride=26), :] = part[:, 0:128]
        pooled[pl.ds(2 * i + 1, 128, stride=26), :] = part[:, 128:256]

    def gather(base, count):
        for j in range(count):
            r = bags[0, 0, order[0, 0, base + j]]
            stage[pl.ds(j, 1), :] = pooled[pl.ds(r, 1), :]
        return stage[0:count, :].astype(BF16)

    def cold_for(k, carry):
        o = lax.rem(s + k, SHARDS)
        send_c[k] = gather(HOT_N + o * PER_COLD, PER_COLD)
        return carry

    lax.fori_loop(0, SHARDS, cold_for, 0)

    pl.semaphore_wait(barrier, SHARDS - 1 + GROUPS - 1 + 3)
    send_pre = remote(pre2.at[0:128], pre2.at[128:256], core_s.at[0], core_r.at[0], partner)
    send_pre.start()
    send_xt = remote(xt.at[1 - core], xt_recv, core_s.at[1], core_r.at[1], partner)
    send_xt.start()

    def cold_to(k, carry):
        o = lax.rem(s + k, SHARDS)
        remote(send_c.at[k], recv_c.at[k], a_s.at[0], a_r.at[0], (g, o)).start()
        remote(meta.at[o], recv_m.at[k], a_s.at[1], a_r.at[1], (g, o)).start()
        return carry

    lax.fori_loop(1, SHARDS, cold_to, 0)
    pltpu.make_async_copy(send_c.at[0], recv_c.at[0], a_r.at[0]).start()
    pltpu.make_async_copy(meta.at[s], recv_m.at[0], a_r.at[1]).start()

    def hot_to(k, carry):
        o = lax.rem(s + k, SHARDS)
        send_h[k] = gather(o * PER_HOT, PER_HOT)
        remote(send_h.at[k], recv_h.at[k], a_s.at[2], a_r.at[2 + k // 8], (g, o)).start()
        return carry

    lax.fori_loop(1, SHARDS, hot_to, 0)
    send_h[0] = gather(s * PER_HOT, PER_HOT)
    pltpu.make_async_copy(send_h.at[0], recv_h.at[0], a_r.at[2]).start()

    send_pre.wait()
    send_xt.wait()
    pre_both = pre2[...]
    for j in range(0, 16, 4):
        both = jnp.concatenate(
            [xt[core, j : j + 4].reshape(4 * PAD_W, 128), xt_recv[j : j + 4].reshape(4 * PAD_W, 128)], axis=1
        )
        part = dot(both, pre_both).astype(BF16)
        for k in range(4):
            w_own[k, j : j + 4] = part[:, k * 128 : (k + 1) * 128].reshape(4, PAD_W, 128)

    right = (zh * 4 + lax.rem(xx + 1, 4), s)
    left = (zh * 4 + lax.rem(xx + 3, 4), s)

    def ring_copy(way, step):
        to = right if way == 0 else left
        if step == 0:
            chunk = lax.rem(xx + 3, 4) if way == 0 else lax.rem(xx + 1, 4)
            src = w_own.at[chunk, pl.ds(way * 8, 8)]
        else:
            src = ring.at[way, step - 1]
        return remote(src, ring.at[way, step], ring_s.at[way, step], ring_r.at[way, step], to)

    def ring_add(way, step):
        chunk = lax.rem(xx + 2 - step, 4) if way == 0 else lax.rem(xx + 2 + step, 4)

        def add(j, carry):
            total = ring[way, step, j].astype(F32) + w_own[chunk, way * 8 + j].astype(F32)
            ring[way, step, j] = total.astype(BF16)
            return carry

        lax.fori_loop(0, 8, add, 0)

    def ring_next(step):
        for way in range(2):
            ring_copy(way, step - 1).wait()
            ring_add(way, step - 1)
            ring_copy(way, step).start()

    for way in range(2):
        ring_copy(way, 0).start()

    load_first.wait()
    load_last.wait()
    eye = zero_one(iota((256, 256), 0) == iota((256, 256), 1))
    first_t[...] = dot_nt(eye, first_ref[...]).astype(BF16)
    turn_row = iota((256, 256), 0)
    turn = zero_one(iota((256, 256), 1) == (turn_row % 32) * 8 + turn_row // 32)
    last_t[...] = dot_nt(turn, last_ref[...]).astype(BF16)
    load_mid.wait()
    block = mid_block[...].astype(F32)
    sub = iota((8, 128), 0) % 4
    apart = (sub + 4 - iota((8, 128), 1) // 32) % 4
    for m0 in range(4):
        for c in range(16):
            value = block[m0 * 8 : (m0 + 1) * 8, c * 128 : (c + 1) * 128]
            out = value
            for d in range(1, 4):
                moved = pltpu.roll(value, 128 - 32 * d, 1)
                moved = jnp.where(sub >= d, pltpu.roll(moved, d, 0), pltpu.roll(moved, d + 4, 0))
                out = jnp.where(apart == d, moved, out)
            row = m0 * 64 + c * 4
            mid_turned[row : row + 4, 0:128] = out[0:4]
            mid_turned[row : row + 4, 128:256] = out[4:8]
    source = turn_row // 64 * 64 + turn_row % 32 * 2 + turn_row // 32 % 2
    midq[...] = dot(zero_one(iota((256, 256), 1) == source), mid_turned[...].astype(BF16)).astype(BF16)
    midl[...] = dot_nt(eye, midq[...]).astype(BF16)
    mid_acc[...] = jnp.zeros_like(mid_acc)

    pltpu.make_async_copy(recv_c, recv_c, a_r.at[0]).wait()
    pltpu.make_async_copy(recv_m, recv_m, a_r.at[1]).wait()

    def words(t, row):
        four = recv_m[pl.ds(4 * t, 4), row : row + 1, :]
        return four[0] + four[1] + four[2] + four[3]

    def pick_cores(u, carry):
        lanes = pl.ds(pl.multiple_of(u * 256, 256), 256)
        both = jnp.concatenate([words(2 * u, 3), words(2 * u + 1, 3)], axis=1)
        for i, (table, out) in enumerate(((first_t, a_t), (last_t, c_t))):
            digit = both % 65536 if i == 0 else both // 65536
            for k in range(4):
                row = iota((256, 256), 0) + k * 256
                onehot[i, k * 256 : (k + 1) * 256, lanes] = zero_one(row == digit)
            part = dot(table[...], onehot[i, :, lanes])
            out[2 * u] = part[:, 0:128]
            out[2 * u + 1] = part[:, 128:256]
        return carry

    lax.fori_loop(0, 4, pick_cores, 0)

    def cold_tile(t, carry):
        lanes = pl.ds(pl.multiple_of(t * 128, 128), 128)
        two = words(t, 0) // 65536
        q_t[...] = recv_c[pl.ds(4 * t, 4)].reshape(128, 128).astype(F32).T
        low = jnp.broadcast_to(jnp.concatenate([two // 8, two // 8], axis=1), (8, 256))
        high = jnp.broadcast_to(jnp.concatenate([two % 8, two % 8], axis=1), (8, 256))
        is_low = [low == k for k in range(4)]
        is_high = [high == k for k in range(8)]

        def packed(mask):
            half = jnp.where(mask, 1.0, 0.0)
            return jnp.concatenate([half, half], axis=0).astype(BF16)

        keep_low = [packed(m) for m in is_low]
        keep_high = [packed(m) for m in is_high]
        for pair in range(4):
            cols = slice(pair * 256, (pair + 1) * 256)
            for e2 in range(2):
                halves = []
                for e3 in (2 * pair, 2 * pair + 1):
                    total = None
                    for e1 in range(8):
                        q_row = e1 * 16 + e2 * 8 + e3
                        term = a_t[t, e1 * 32 : (e1 + 1) * 32, :] * q_t[q_row : q_row + 1, :]
                        total = term if total is None else total + term
                    halves.append(total)
                h = jnp.concatenate(halves, axis=1).astype(BF16).reshape(2, 16, 256)
                for k in range(4):
                    he[k * 64 + e2 * 32 : k * 64 + e2 * 32 + 32, cols] = (h * keep_low[k][None]).reshape(32, 256)
            c = jnp.concatenate(
                [c_t[t, e3 * 32 : (e3 + 1) * 32, :] for e3 in (2 * pair, 2 * pair + 1)], axis=1
            )
            c = c.astype(BF16).reshape(2, 16, 256)
            for k in range(8):
                ce[k * 32 : (k + 1) * 32, cols] = (c * keep_high[k][None]).reshape(32, 256)
            q_all = dot(midq[...], ce[:, cols]).reshape(4, 8, 8, 256)
            total = q_all[0]
            for k in range(1, 4):
                total = jnp.where(is_low[k][None], q_all[k], total)
            qs[:, cols] = total.reshape(64, 256)
            l_all = dot(midl[...], he[:, cols]).reshape(8, 4, 8, 256)
            total = l_all[0]
            for k in range(1, 8):
                total = jnp.where(is_high[k][None], l_all[k], total)
            total = total.reshape(32, 256).astype(BF16)
            tl[pair * 64 : pair * 64 + 32, lanes] = total[:, 0:128]
            tl[pair * 64 + 32 : pair * 64 + 64, lanes] = total[:, 128:256]
        mid_acc[...] += dot_nt(he[...], ce[...])
        for e1 in range(8):
            total = None
            for e2 in range(2):
                for e3 in range(8):
                    q_row = e1 * 16 + e2 * 8 + e3
                    term = qs[e2 * 32 : (e2 + 1) * 32, e3 * 128 : (e3 + 1) * 128] * q_t[q_row : q_row + 1, :]
                    total = term if total is None else total + term
            row = (e1 % 4) * 64 + (e1 // 4) * 32
            tf[row : row + 32, lanes] = total.astype(BF16)
        return carry

    ring_next(1)
    lax.fori_loop(0, 5, cold_tile, 0)
    ring_next(2)
    lax.fori_loop(5, 8, cold_tile, 0)

    row = iota((256, 256), 0)
    j = row % 32
    source = (j % 8) * 32 + ((row // 32 % 2) * 4 + row // 64) * 4 + j // 8
    tl[...] = dot(zero_one(iota((256, 256), 1) == source), tl[...]).astype(BF16)
    lane = iota((256, 128), 1)

    def by_digit(k, carry):
        rows = pl.ds(pl.multiple_of(k * 256, 256), 256)
        one = dot_nt(onehot[0, rows, :], tf[...])
        two = dot_nt(onehot[1, rows, :], tl[...])
        for i in range(4):
            a = one[:, i // 2 * 128 : i // 2 * 128 + 128]
            b = two[:, i // 2 * 128 : i // 2 * 128 + 128]
            if i % 2 == 0:
                part = jnp.where(lane < 64, a, pltpu.roll(b, 64, 1))
            else:
                part = jnp.where(lane < 64, pltpu.roll(a, 64, 1), b)
            for n in range(8):
                fl_own[n % 2, i, 4 * k + n // 2] = part[n * 32 : (n + 1) * 32, :]
        return carry

    lax.fori_loop(0, 4, by_digit, 0)

    def fl_round(j, carry):
        for i in range(4):
            fl_send[i, j] = fl_own[1 - core, i, j].astype(BF16)
        return carry

    lax.fori_loop(0, 16, fl_round, 0)
    fl_copy = remote(fl_send, fl_recv, core_s.at[2], core_r.at[2], partner)
    fl_copy.start()

    row = iota((256, 256), 0)
    source = (row % 4) * 64 + (row // 4 % 2) * 32 + ((row // 32 % 2) * 4 + row // 64) * 4 + row // 8 % 4
    moved = dot(zero_one(iota((256, 256), 1) == source), mid_acc[...].astype(BF16)).astype(BF16)
    for k in range(8):
        mid_send[k] = moved[k * 32 : (k + 1) * 32, :]

    def mid_copy(d):
        to = lax.rem(g + d, GROUPS)
        src = mid_send.at[lax.rem(to, 4) * 2 + to // 4]
        return remote(src, mid_recv.at[d - 1], m_s.at[d - 1], m_r.at[d - 1], (to, s))

    for d in range(1, GROUPS):
        mid_copy(d).start()

    for way in range(2):
        ring_copy(way, 2).wait()

        def last_add(j, carry):
            total = ring[way, 2, j].astype(F32) + w_own[xx, way * 8 + j].astype(F32)
            wy[way * 8 + j] = total.astype(BF16)
            return carry

        lax.fori_loop(0, 8, last_add, 0)

    def y_copy(buf, into, send_sem, recv_sem, d):
        to = lax.rem(yy + d, 4)
        src = buf.at[pl.ds(4 * to, 4)]
        return remote(src, into.at[d - 1], send_sem.at[d - 1], recv_sem.at[d - 1], (g, shard_at(to, zl, core)))

    for d in range(1, 4):
        y_copy(wy, wy_recv, wy_s, wy_r, d).start()

    fl_copy.wait()
    for y in range(4):
        for z in range(4):
            for k in range(4):
                total = fl_own[core, k, 4 * y + z] + fl_recv[k, 4 * y + z].astype(F32)
                if z < 2:
                    fa[k, y, z] = total.astype(BF16)
                else:
                    fb[y, k, z - 2] = total.astype(BF16)

    def f_copy(n, d):
        by_x = n in (0, 3)
        to = lax.rem((xx if by_x else yy) + d, 4)
        device = (zh * 4 + to, s) if by_x else (g, shard_at(to, zl, core))
        buf, into = ((fa, fa_recv), (fb, fb_recv), (fa2, fa2_recv), (fb2, fb2_recv))[n]
        return remote(buf.at[to], into.at[d - 1], f_s.at[n, d - 1], f_r.at[n, d - 1], device)

    for d in range(1, 4):
        f_copy(0, d).start()
        f_copy(1, d).start()

    hot[...] = jnp.zeros_like(hot)

    def hot_part(i, carry):
        ids = []
        for half in range(2):
            four = recv_m[pl.ds(8 * i + 4 * half, 4), :, :]
            four = four[0] + four[1] + four[2] + four[3]
            ids += [four[k : k + 1, :] % 65536 for k in range(3)]
        values = recv_h[pl.ds(8 * i, 8)].reshape(768, 128).astype(F32)
        low = jnp.concatenate(ids, axis=1) % 512
        pick = zero_one(iota((512, 768), 0) == low)
        column = jnp.concatenate(
            [jnp.broadcast_to((r // 512).astype(F32), (128, 128)).T for r in ids], axis=0
        )
        for k in range(0, 4, 2):
            both = [jnp.where(column == float(k + n), values, 0.0).astype(BF16) for n in range(2)]
            part = dot(pick, jnp.concatenate(both, axis=1))
            hot[k * 512 : (k + 1) * 512, :] += part[:, 0:128]
            hot[(k + 1) * 512 : (k + 2) * 512, :] += part[:, 128:256]
        return carry

    def hot_group(i):
        some = recv_h.at[8 * i : 8 * i + 8]
        pltpu.make_async_copy(some, some, a_r.at[2 + i]).wait()
        hot_part(i, 0)

    hot_group(0)
    hot_group(1)

    for d in range(1, 4):
        f_copy(0, d).wait()
    for n in range(4):
        for z in range(2):
            total = fa[xx, n, z].astype(F32)
            for d in range(3):
                total = total + fa_recv[d, n, z].astype(F32)
            fa2[n, z] = total.astype(BF16)
    for d in range(1, 4):
        f_copy(2, d).start()
    for d in range(1, 4):
        f_copy(1, d).wait()
    for n in range(4):
        for z in range(2):
            total = fb[yy, n, z].astype(F32)
            for d in range(3):
                total = total + fb_recv[d, n, z].astype(F32)
            fb2[n, z] = total.astype(BF16)
    for d in range(1, 4):
        f_copy(3, d).start()

    for d in range(1, 4):
        y_copy(wy, wy_recv, wy_s, wy_r, d).wait()

    def halves(total, count, width):
        top, bottom = total[0:count], total[count : 2 * count]
        left_half = iota((count, 128), 1) % (2 * width) < width
        return (
            jnp.where(left_half, top, pltpu.roll(bottom, width, 1)),
            jnp.where(left_half, pltpu.roll(top, 128 - width, 1), bottom),
        )

    def z_copy(buf, into, send_sem, recv_sem, d):
        to, device = along_z(d)
        return remote(buf.at[to], into.at[d - 1], send_sem.at[d - 1], recv_sem.at[d - 1], device)

    for j in range(4):
        total = wy[4 * yy + j].astype(F32)
        for d in range(3):
            total = total + wy_recv[d, j].astype(F32)
        for k, half in enumerate(halves(total, 56, 64)):
            wz[4 * k + j] = jnp.concatenate([half, jnp.zeros((8, 128), F32)], axis=0).astype(BF16)
    for d in range(1, 8):
        z_copy(wz, wz_recv, wz_s, wz_r, d).start()

    hot_group(2)

    for d in range(1, 4):
        f_copy(2, d).wait()
        f_copy(3, d).wait()
    for j in range(4):
        buf, into, at = (fa2, fa2_recv, yy) if j < 2 else (fb2, fb2_recv, xx)
        total = buf[at, j % 2].astype(F32)
        for d in range(3):
            total = total + into[d, j % 2].astype(F32)
        for k, half in enumerate(halves(total, 16, 32)):
            fz[4 * k + j] = half.astype(BF16)
    for d in range(1, 8):
        z_copy(fz, fz_recv, fz_s, fz_r, d).start()

    hot_group(3)
    save_hot = pltpu.make_async_copy(hot, hot_hbm, load_s.at[6])
    save_hot.start()

    for d in range(1, GROUPS):
        mid_copy(d).wait()
    total = mid_send[xx * 2 + zh].astype(F32)
    for d in range(GROUPS - 1):
        total = total + mid_recv[d].astype(F32)
    mout_ref[...] = total

    for d in range(1, 8):
        z_copy(wz, wz_recv, wz_s, wz_r, d).wait()
    total = wz[deep].astype(F32)
    for d in range(7):
        total = total + wz_recv[d].astype(F32)
    wout_ref[0:56, :] = total[0:56]
    wout_ref[56:PAD_W, :] = pltpu.roll(total, 64, 1)[0:56]
    wout_ref[PAD_W:128, :] = jnp.zeros((128 - PAD_W, 128), F32)

    for d in range(1, 8):
        z_copy(fz, fz_recv, fz_s, fz_r, d).wait()
    total = fz[deep].astype(F32)
    for d in range(7):
        total = total + fz_recv[d].astype(F32)
    fout_ref[0:16, :] = total[:, 0:32]
    fout_ref[16:32, :] = pltpu.roll(total, 96, 1)[:, 0:32]
    lout_ref[0:16, :] = pltpu.roll(total, 64, 1)[:, 0:32]
    lout_ref[16:32, :] = pltpu.roll(total, 32, 1)[:, 0:32]

    save_hot.wait()
    sent = send_c.at[pl.ds(1, SHARDS - 1)]
    pltpu.make_async_copy(sent, sent, a_s.at[0]).wait()
    sent = recv_m.at[pl.ds(1, SHARDS - 1)]
    pltpu.make_async_copy(sent, sent, a_s.at[1]).wait()
    sent = send_h.at[pl.ds(1, SHARDS - 1)]
    pltpu.make_async_copy(sent, sent, a_s.at[2]).wait()


def finish(dense, hot, weight, first, last, mid, dense_out, hot_out, weight_out, first_out, last_out, mid_out):
    dense_out[...] = dense[...]
    hot_out[...] = hot[...]
    weight_out[...] = weight[...].T[0:64, 0:BLOCK_W]
    first_out[...] = first[...]
    last_out[...] = last[...]
    for m1 in range(8):
        parts = []
        for a in range(4):
            for e2 in range(2):
                row = a * 8 + e2 * 4
                parts.append(mid[row : row + 4, m1 * 32 : (m1 + 1) * 32])
        rows = jnp.concatenate(parts, axis=1)
        for m0 in range(4):
            mid_out[m0 * 8 + m1 : m0 * 8 + m1 + 1, :] = rows[m0 : m0 + 1, :]


def body(
    top_input,
    pre_act,
    grad_hidden,
    top_weight,
    core_first,
    core_mid,
    core_last,
    bag_ids,
    lookup_order,
    hot_rows,
    cold_digits,
):
    vmem = pl.BlockSpec(memory_space=pltpu.VMEM)
    smem = pl.BlockSpec(memory_space=pltpu.SMEM)
    hbm = pl.BlockSpec(memory_space=pl.ANY)

    def buf(*shape, dtype=BF16):
        return pltpu.VMEM(shape, dtype)

    dma = pltpu.SemaphoreType.DMA
    shapes = (
        jax.ShapeDtypeStruct((128, 128), BF16),
        jax.ShapeDtypeStruct((2048, 128), F32),
        jax.ShapeDtypeStruct((128, 128), F32),
        jax.ShapeDtypeStruct((32, 32), F32),
        jax.ShapeDtypeStruct((32, 32), F32),
        jax.ShapeDtypeStruct((32, 256), F32),
    )
    outs = pl.pallas_call(
        kernel,
        out_shape=shapes,
        in_specs=[hbm, hbm, hbm, hbm, smem, smem, vmem, vmem, hbm, hbm, hbm],
        out_specs=(vmem, hbm, vmem, vmem, vmem, vmem),
        scratch_shapes=[
            buf(128, 512),
            buf(128, 512),
            buf(3456, 512),
            buf(128, 3456),
            buf(1024, 256),
            buf(1024, 256),
            buf(32, 2048),
            buf(256, 256, dtype=F32),
            buf(256, 256),
            buf(256, 256),
            buf(2048, 128, dtype=F32),
            buf(26 * 128, 128, dtype=F32),
            buf(PER_HOT, 128, dtype=F32),
            buf(SHARDS, 4, 128, dtype=I32),
            buf(SHARDS, PER_COLD, 128),
            buf(SHARDS, PER_HOT, 128),
            buf(SHARDS, PER_COLD, 128),
            buf(SHARDS, PER_HOT, 128),
            buf(SHARDS, 4, 128, dtype=I32),
            buf(2, 16, PAD_W, 128),
            buf(16, PAD_W, 128),
            buf(256, 512),
            buf(4, 16, PAD_W, 128),
            buf(2, 3, 8, PAD_W, 128),
            buf(256, 1024),
            buf(256, 1024),
            buf(2, 1024, 1024),
            buf(8, 256, 128, dtype=F32),
            buf(8, 256, 128, dtype=F32),
            buf(128, 128, dtype=F32),
            buf(256, 1024),
            buf(256, 1024),
            buf(64, 1024, dtype=F32),
            buf(256, 1024),
            buf(256, 1024),
            buf(256, 256, dtype=F32),
            buf(8, 32, 256),
            buf(7, 32, 256),
            buf(2, 4, 16, 32, 128, dtype=F32),
            buf(4, 16, 32, 128),
            buf(4, 16, 32, 128),
            buf(4, 4, 2, 32, 128),
            buf(3, 4, 2, 32, 128),
            buf(4, 4, 2, 32, 128),
            buf(3, 4, 2, 32, 128),
            buf(4, 2, 32, 128),
            buf(3, 2, 32, 128),
            buf(4, 2, 32, 128),
            buf(3, 2, 32, 128),
            buf(16, PAD_W, 128),
            buf(3, 4, PAD_W, 128),
            buf(8, 64, 128),
            buf(7, 64, 128),
            buf(8, 16, 128),
            buf(7, 16, 128),
            dma((8,)),
            dma((3,)),
            dma((3,)),
            dma((3,)),
            dma((6,)),
            dma((2, 3)),
            dma((2, 3)),
            dma((4, 3)),
            dma((4, 3)),
            dma((3,)),
            dma((3,)),
            dma((7,)),
            dma((7,)),
            dma((7,)),
            dma((7,)),
            dma((7,)),
            dma((7,)),
        ],
        compiler_params=pltpu.CompilerParams(
            collective_id=0, has_side_effects=True, vmem_limit_bytes=56 * 1024 * 1024
        ),
    )(
        pre_act,
        grad_hidden,
        top_weight,
        top_input,
        bag_ids,
        lookup_order,
        hot_rows.reshape(24, 128),
        cold_digits.reshape(24, 128),
        core_first,
        core_last,
        core_mid,
    )
    dense_grad, hot_grad, weight_grad, first_grad, last_grad, mid_grad = pl.pallas_call(
        finish,
        out_shape=shapes[:2] + (jax.ShapeDtypeStruct((64, BLOCK_W), F32),) + shapes[3:],
        in_specs=[vmem] * 6,
        out_specs=(vmem,) * 6,
    )(*outs)
    return (hot_grad[None], dense_grad, weight_grad.T, first_grad, mid_grad, last_grad)


def solution(mesh):
    return jax.shard_map(
        body,
        mesh=mesh,
        in_specs=(
            P(("group", "shard"), None),
            P(("group", "shard"), None),
            P(("group", "shard"), None),
            P(),
            P(),
            P(),
            P(),
            P("group", "shard", None),
            P("group", "shard", None),
            P("group", "shard", None),
            P("group", "shard", None, None),
        ),
        out_specs=(
            P("group", "shard", None),
            P(("group", "shard"), None),
            P("shard", "group"),
            P("shard", "group"),
            P("shard", "group"),
            P("shard", "group"),
        ),
        check_vma=False,
    )
```

```python
import functools

import jax
import jax.numpy as jnp
from jax import lax
from jax.experimental import pallas as pl
from jax.experimental.pallas import tpu as pltpu
from jax.sharding import PartitionSpec as P

F32 = jnp.float32
BF16 = jnp.bfloat16
I32 = jnp.int32

E = 128
RANK = 32
E1 = 8
E2 = 2
E3 = 8
HOT_N = 3072
SHARDS = 32
GROUPS = 8
PER_HOT = 96
PER_COLD = 32
BLOCK_W = 108
PAD_W = 112
ROWS = PAD_W + 32
MESH = pl.DeviceIdType.MESH


def iota(shape, dim):
    return lax.broadcasted_iota(I32, shape, dim)


def dot(a, b):
    return jnp.dot(a, b, preferred_element_type=F32)


def dot_nt(a, b):
    return lax.dot_general(a, b, (((1,), (1,)), ((), ())), preferred_element_type=F32)


def zero_one(mask):
    return jnp.where(mask, 1.0, 0.0).astype(BF16)


def kernel(
    act_hbm, hid_hbm, tw_hbm, x_hbm, bags, order, hot_in, dig_in, first_hbm, last_hbm, mid_hbm,
    dense_ref, hot_hbm, wout_ref, fout_ref, lout_ref, mout_ref,
    act_ref, hid_ref, tw_ref, x_ref, first_ref, last_ref, mid_block, mid_turned, midq, midl, hot,
    pooled, stage, meta, send_c, send_h, recv_c, recv_h, recv_m,
    xt, xt_recv, pre2, w_own, ring,
    first_t, last_t, onehot, a_t, c_t, q_t, he, ce, qs, tf, tl, mid_acc, mid_send, mid_recv,
    fl_own, fl_send, fl_recv, fx, fx_sum, fx_recv,
    wy, wy_recv, wz, wz_recv, fz, fz_recv,
    load_s, core_s, core_r, a_s, a_r, ring_s, ring_r, f_s, f_r, wy_s, wy_r, wz_s, wz_r,
    fz_s, fz_r, m_s, m_r,
):
    g = lax.axis_index("group")
    s = lax.axis_index("shard")
    xx = lax.rem(g, 4)
    zh = g // 4
    core = lax.rem(s, 2)
    zl = lax.rem(s // 2, 4)
    yy = s // 8
    deep = zh * 4 + zl

    load_act = pltpu.make_async_copy(act_hbm, act_ref, load_s.at[0])
    load_hid = pltpu.make_async_copy(hid_hbm, hid_ref, load_s.at[1])
    load_x = pltpu.make_async_copy(x_hbm, x_ref, load_s.at[2])
    load_tw = pltpu.make_async_copy(tw_hbm, tw_ref, load_s.at[3])
    load_first = pltpu.make_async_copy(first_hbm, first_ref, load_s.at[4])
    load_last = pltpu.make_async_copy(last_hbm, last_ref, load_s.at[5])
    load_mid = pltpu.make_async_copy(mid_hbm.at[pl.ds(pl.multiple_of(s * 32, 32), 32)], mid_block, load_s.at[7])
    load_act.start()
    load_hid.start()
    load_x.start()
    load_tw.start()
    load_first.start()
    load_last.start()
    load_mid.start()

    def shard_at(y, z, c):
        return y * 8 + z * 2 + c

    def remote(src, dst, send_sem, recv_sem, to):
        return pltpu.make_async_remote_copy(
            src_ref=src, dst_ref=dst, send_sem=send_sem, recv_sem=recv_sem, device_id=to, device_id_type=MESH
        )

    def along_z(d):
        to = lax.rem(deep + d, 8)
        return to, ((to // 4) * 4 + xx, shard_at(yy, lax.rem(to, 4), core))

    partner = (g, shard_at(yy, zl, 1 - core))

    barrier = pltpu.get_barrier_semaphore()

    def greet_shard(k, carry):
        pl.semaphore_signal(barrier, inc=1, device_id=(g, lax.rem(s + k, SHARDS)), device_id_type=MESH)
        return carry

    def greet_group(k, carry):
        pl.semaphore_signal(barrier, inc=1, device_id=(lax.rem(g + k, GROUPS), s), device_id_type=MESH)
        return carry

    def greet_far(k, carry):
        to = lax.rem(yy * 4 + zl + k, 16)
        to = (lax.rem(g + 4, 8), shard_at(to // 4, lax.rem(to, 4), core))
        pl.semaphore_signal(barrier, inc=1, device_id=to, device_id_type=MESH)
        return carry

    lax.fori_loop(1, SHARDS, greet_shard, 0)
    lax.fori_loop(1, GROUPS, greet_group, 0)
    lax.fori_loop(1, 16, greet_far, 0)

    turns = lax.rem(s, 4)

    def turned(values, width):
        out = values
        for n in range(1, 4):
            out = jnp.where(turns == n, pltpu.roll(values, (4 - n) * width, 1), out)
        return out

    def kept(values, width, i):
        low = lax.rem(i + 4 - turns, 4) * width
        lane = iota(values.shape, 1)
        return jnp.where((lane >= low) & (lane < low + width), values, 0)

    hots = turned(jnp.concatenate([hot_in[pl.ds(c, 8, stride=3), :] for c in range(3)], axis=1), PER_HOT)
    one_three = turned(dig_in[0:8, :] + dig_in[16:24, :] * 65536, PER_COLD)
    two = turned(dig_in[8:16, :] % 32 * 65536, PER_COLD)
    for i in range(4):
        hot_i = kept(hots, PER_HOT, i)
        rows = [hot_i[:, c * 128 : (c + 1) * 128] for c in range(3)] + [kept(one_three, PER_COLD, i)]
        rows[0] = rows[0] + kept(two, PER_COLD, i)
        for q in range(8):
            for c in range(4):
                meta[4 * q + i, c : c + 1, :] = rows[c][q : q + 1, :]

    load_act.wait()
    load_hid.wait()
    pre = jnp.where(act_ref[...].astype(F32) > 0, hid_ref[...].astype(F32), 0.0).astype(BF16)
    col = iota((512, 512), 1)
    source = (col // 64 % 2) * 256 + (col // 128) * 64 + col % 64
    pre2[0:128, :] = dot(pre, zero_one(iota((512, 512), 0) == source)).astype(BF16)

    load_x.wait()
    for shard in range(SHARDS):
        lo = shard * BLOCK_W // 128 * 128
        off = shard * BLOCK_W - lo
        width = 128 if off + BLOCK_W <= 128 else 256
        pick = zero_one(iota((PAD_W, width), 1) == iota((PAD_W, width), 0) + off)
        xt[shard % 2, shard // 2] = dot_nt(pick, x_ref[:, lo : lo + width]).astype(BF16)

    load_tw.wait()
    dense_ref[...] = dot_nt(pre, tw_ref[0:128, :]).astype(BF16)
    for i in range(13):
        part = dot_nt(pre, tw_ref[128 + i * 256 : 384 + i * 256, :]).astype(BF16).astype(F32)
        pooled[pl.ds(2 * i, 128, stride=26), :] = part[:, 0:128]
        pooled[pl.ds(2 * i + 1, 128, stride=26), :] = part[:, 128:256]

    def gather(base, count):
        for j in range(count):
            r = bags[0, 0, order[0, 0, base + j]]
            stage[pl.ds(j, 1), :] = pooled[pl.ds(r, 1), :]
        return stage[0:count, :].astype(BF16)

    def cold_for(k, carry):
        o = lax.rem(s + k, SHARDS)
        send_c[k] = gather(HOT_N + o * PER_COLD, PER_COLD)
        return carry

    lax.fori_loop(0, SHARDS, cold_for, 0)

    def hot_for(k, carry):
        o = lax.rem(s + k, SHARDS)
        send_h[k] = gather(o * PER_HOT, PER_HOT)
        return carry

    lax.fori_loop(0, SHARDS, hot_for, 0)

    pl.semaphore_wait(barrier, SHARDS - 1 + GROUPS - 1 + 15)
    send_pre = remote(pre2.at[0:128], pre2.at[128:256], core_s.at[0], core_r.at[0], partner)
    send_pre.start()
    send_xt = remote(xt.at[1 - core], xt_recv, core_s.at[1], core_r.at[1], partner)
    send_xt.start()

    def cold_to(k, carry):
        o = lax.rem(s + k, SHARDS)
        remote(send_c.at[k], recv_c.at[k], a_s.at[0], a_r.at[0], (g, o)).start()
        remote(meta.at[o], recv_m.at[k], a_s.at[1], a_r.at[1], (g, o)).start()
        return carry

    lax.fori_loop(1, SHARDS, cold_to, 0)
    pltpu.make_async_copy(send_c.at[0], recv_c.at[0], a_r.at[0]).start()
    pltpu.make_async_copy(meta.at[s], recv_m.at[0], a_r.at[1]).start()

    send_pre.wait()
    send_xt.wait()
    pre_both = pre2[...]
    for j in range(0, 16, 4):
        both = jnp.concatenate(
            [xt[core, j : j + 4].reshape(4 * PAD_W, 128), xt_recv[j : j + 4].reshape(4 * PAD_W, 128)], axis=1
        )
        part = dot(both, pre_both).astype(BF16)
        for k in range(4):
            w_own[k, j : j + 4] = part[:, k * 128 : (k + 1) * 128].reshape(4, PAD_W, 128)

    right = (zh * 4 + lax.rem(xx + 1, 4), s)
    left = (zh * 4 + lax.rem(xx + 3, 4), s)

    def ring_copy(way, step):
        to = right if way == 0 else left
        if step == 0:
            chunk = lax.rem(xx + 3, 4) if way == 0 else lax.rem(xx + 1, 4)
            src = w_own.at[chunk, pl.ds(way * 8, 8)]
        else:
            src = ring.at[way, step - 1]
        return remote(src, ring.at[way, step], ring_s.at[way, step], ring_r.at[way, step], to)

    def ring_add(way, step):
        chunk = lax.rem(xx + 2 - step, 4) if way == 0 else lax.rem(xx + 2 + step, 4)

        def add(j, carry):
            total = ring[way, step, j].astype(F32) + w_own[chunk, way * 8 + j].astype(F32)
            ring[way, step, j] = total.astype(BF16)
            return carry

        lax.fori_loop(0, 8, add, 0)

    def ring_next(step):
        for way in range(2):
            ring_copy(way, step - 1).wait()
            ring_add(way, step - 1)
            ring_copy(way, step).start()

    for way in range(2):
        ring_copy(way, 0).start()

    def hot_to(k, carry):
        o = lax.rem(s + k, SHARDS)
        remote(send_h.at[k], recv_h.at[k], a_s.at[2], a_r.at[2 + k // 8], (g, o)).start()
        return carry

    lax.fori_loop(1, 4, hot_to, 0)
    pltpu.make_async_copy(send_h.at[0], recv_h.at[0], a_r.at[2]).start()

    load_first.wait()
    load_last.wait()
    eye = zero_one(iota((256, 256), 0) == iota((256, 256), 1))
    first_t[...] = dot_nt(eye, first_ref[...]).astype(BF16)
    turn_row = iota((256, 256), 0)
    turn = zero_one(iota((256, 256), 1) == (turn_row % 32) * 8 + turn_row // 32)
    last_t[...] = dot_nt(turn, last_ref[...]).astype(BF16)
    load_mid.wait()
    block = mid_block[...].astype(F32)
    sub = iota((8, 128), 0) % 4
    apart = (sub + 4 - iota((8, 128), 1) // 32) % 4
    for m0 in range(4):
        for c in range(16):
            value = block[m0 * 8 : (m0 + 1) * 8, c * 128 : (c + 1) * 128]
            out = value
            for d in range(1, 4):
                moved = pltpu.roll(value, 128 - 32 * d, 1)
                moved = jnp.where(sub >= d, pltpu.roll(moved, d, 0), pltpu.roll(moved, d + 4, 0))
                out = jnp.where(apart == d, moved, out)
            row = m0 * 64 + c * 4
            mid_turned[row : row + 4, 0:128] = out[0:4]
            mid_turned[row : row + 4, 128:256] = out[4:8]
    source = turn_row // 64 * 64 + turn_row % 32 * 2 + turn_row // 32 % 2
    midq[...] = dot(zero_one(iota((256, 256), 1) == source), mid_turned[...].astype(BF16)).astype(BF16)
    midl[...] = dot_nt(eye, midq[...]).astype(BF16)
    mid_acc[...] = jnp.zeros_like(mid_acc)

    pltpu.make_async_copy(recv_c, recv_c, a_r.at[0]).wait()
    pltpu.make_async_copy(recv_m, recv_m, a_r.at[1]).wait()

    def words(t, row):
        four = recv_m[pl.ds(4 * t, 4), row : row + 1, :]
        return four[0] + four[1] + four[2] + four[3]

    def pick_cores(u, carry):
        lanes = pl.ds(pl.multiple_of(u * 256, 256), 256)
        both = jnp.concatenate([words(2 * u, 3), words(2 * u + 1, 3)], axis=1)
        for i, (table, out) in enumerate(((first_t, a_t), (last_t, c_t))):
            digit = both % 65536 if i == 0 else both // 65536
            for k in range(4):
                row = iota((256, 256), 0) + k * 256
                onehot[i, k * 256 : (k + 1) * 256, lanes] = zero_one(row == digit)
            part = dot(table[...], onehot[i, :, lanes])
            out[2 * u] = part[:, 0:128]
            out[2 * u + 1] = part[:, 128:256]
        return carry

    lax.fori_loop(0, 4, pick_cores, 0)

    def cold_tile(t, carry):
        lax.fori_loop(4 * t + 4, jnp.minimum(4 * t + 8, SHARDS), hot_to, 0)
        lanes = pl.ds(pl.multiple_of(t * 128, 128), 128)
        two = words(t, 0) // 65536
        q_t[...] = recv_c[pl.ds(4 * t, 4)].reshape(128, 128).astype(F32).T
        low = jnp.broadcast_to(jnp.concatenate([two // 8, two // 8], axis=1), (8, 256))
        high = jnp.broadcast_to(jnp.concatenate([two % 8, two % 8], axis=1), (8, 256))
        is_low = [low == k for k in range(4)]
        is_high = [high == k for k in range(8)]

        def packed(mask):
            half = jnp.where(mask, 1.0, 0.0)
            return jnp.concatenate([half, half], axis=0).astype(BF16)

        keep_low = [packed(m) for m in is_low]
        keep_high = [packed(m) for m in is_high]
        for pair in range(4):
            cols = slice(pair * 256, (pair + 1) * 256)
            for e2 in range(2):
                halves = []
                for e3 in (2 * pair, 2 * pair + 1):
                    total = None
                    for e1 in range(8):
                        q_row = e1 * 16 + e2 * 8 + e3
                        term = a_t[t, e1 * 32 : (e1 + 1) * 32, :] * q_t[q_row : q_row + 1, :]
                        total = term if total is None else total + term
                    halves.append(total)
                h = jnp.concatenate(halves, axis=1).astype(BF16).reshape(2, 16, 256)
                for k in range(4):
                    he[k * 64 + e2 * 32 : k * 64 + e2 * 32 + 32, cols] = (h * keep_low[k][None]).reshape(32, 256)
            c = jnp.concatenate(
                [c_t[t, e3 * 32 : (e3 + 1) * 32, :] for e3 in (2 * pair, 2 * pair + 1)], axis=1
            )
            c = c.astype(BF16).reshape(2, 16, 256)
            for k in range(8):
                ce[k * 32 : (k + 1) * 32, cols] = (c * keep_high[k][None]).reshape(32, 256)
            q_all = dot(midq[...], ce[:, cols]).reshape(4, 8, 8, 256)
            total = q_all[0]
            for k in range(1, 4):
                total = jnp.where(is_low[k][None], q_all[k], total)
            qs[:, cols] = total.reshape(64, 256)
            l_all = dot(midl[...], he[:, cols]).reshape(8, 4, 8, 256)
            total = l_all[0]
            for k in range(1, 8):
                total = jnp.where(is_high[k][None], l_all[k], total)
            total = total.reshape(32, 256).astype(BF16)
            tl[pair * 64 : pair * 64 + 32, lanes] = total[:, 0:128]
            tl[pair * 64 + 32 : pair * 64 + 64, lanes] = total[:, 128:256]
        mid_acc[...] += dot_nt(he[...], ce[...])
        for e1 in range(8):
            total = None
            for e2 in range(2):
                for e3 in range(8):
                    q_row = e1 * 16 + e2 * 8 + e3
                    term = qs[e2 * 32 : (e2 + 1) * 32, e3 * 128 : (e3 + 1) * 128] * q_t[q_row : q_row + 1, :]
                    total = term if total is None else total + term
            row = (e1 % 4) * 64 + (e1 // 4) * 32
            tf[row : row + 32, lanes] = total.astype(BF16)
        return carry

    ring_next(1)
    lax.fori_loop(0, 6, cold_tile, 0)
    ring_next(2)
    lax.fori_loop(6, 8, cold_tile, 0)

    row = iota((256, 256), 0)
    j = row % 32
    source = (j % 8) * 32 + ((row // 32 % 2) * 4 + row // 64) * 4 + j // 8
    tl[...] = dot(zero_one(iota((256, 256), 1) == source), tl[...]).astype(BF16)
    lane = iota((256, 128), 1)

    def by_digit(k, carry):
        rows = pl.ds(pl.multiple_of(k * 256, 256), 256)
        one = dot_nt(onehot[0, rows, :], tf[...])
        two = dot_nt(onehot[1, rows, :], tl[...])
        for i in range(4):
            a = one[:, i // 2 * 128 : i // 2 * 128 + 128]
            b = two[:, i // 2 * 128 : i // 2 * 128 + 128]
            if i % 2 == 0:
                part = jnp.where(lane < 64, a, pltpu.roll(b, 64, 1))
            else:
                part = jnp.where(lane < 64, pltpu.roll(a, 64, 1), b)
            for n in range(8):
                block = part[n * 32 : (n + 1) * 32, :]
                fl_own[n % 2, i, 4 * k + n // 2] = block
                fl_send[n % 2, i, 4 * k + n // 2] = block.astype(BF16)
        return carry

    lax.fori_loop(0, 4, by_digit, 0)

    fl_copy = remote(fl_send.at[1 - core], fl_recv, core_s.at[2], core_r.at[2], partner)
    fl_copy.start()

    row = iota((256, 256), 0)
    source = (row % 4) * 64 + (row // 4 % 2) * 32 + ((row // 32 % 2) * 4 + row // 64) * 4 + row // 8 % 4
    moved = dot(zero_one(iota((256, 256), 1) == source), mid_acc[...].astype(BF16)).astype(BF16)
    for k in range(8):
        mid_send[k] = moved[k * 32 : (k + 1) * 32, :]

    def mid_copy(d):
        to = lax.rem(g + d, GROUPS)
        src = mid_send.at[lax.rem(to, 4) * 2 + to // 4]
        return remote(src, mid_recv.at[d - 1], m_s.at[d - 1], m_r.at[d - 1], (to, s))

    for d in range(1, GROUPS):
        mid_copy(d).start()

    for way in range(2):
        ring_copy(way, 2).wait()

        def last_add(j, carry):
            total = ring[way, 2, j].astype(F32) + w_own[xx, way * 8 + j].astype(F32)
            wy[way * 8 + j] = total.astype(BF16)
            return carry

        lax.fori_loop(0, 8, last_add, 0)

    def y_copy(buf, into, send_sem, recv_sem, d):
        to = lax.rem(yy + d, 4)
        src = buf.at[pl.ds(4 * to, 4)]
        return remote(src, into.at[d - 1], send_sem.at[d - 1], recv_sem.at[d - 1], (g, shard_at(to, zl, core)))

    for d in range(1, 4):
        y_copy(wy, wy_recv, wy_s, wy_r, d).start()

    fl_copy.wait()

    def fl_pair(j, carry):
        for k in range(4):
            fx[k, j] = (fl_own[core, k, j] + fl_recv[k, j].astype(F32)).astype(BF16)
        return carry

    lax.fori_loop(0, 16, fl_pair, 0)
    next_x = (lax.rem(xx + 1, 4), lax.rem(xx + 3, 4))
    far_x = lax.rem(xx + 2, 4)
    low_half, high_half = pl.ds(0, 8), pl.ds(8, 8)

    def f_copy(n):
        way = n % 2
        half = (low_half, high_half)[way]
        rest = (high_half, low_half)[way]
        src = (fx.at[far_x, half], fx.at[next_x[way], rest], fx_sum.at[way])[n // 2]
        return remote(src, fx_recv.at[n], f_s.at[n], f_r.at[n], (right, left)[way])

    for n in range(4):
        f_copy(n).start()

    hot[...] = jnp.zeros_like(hot)

    def hot_part(i, carry):
        ids = []
        for half in range(2):
            four = recv_m[pl.ds(8 * i + 4 * half, 4), :, :]
            four = four[0] + four[1] + four[2] + four[3]
            ids += [four[k : k + 1, :] % 65536 for k in range(3)]
        values = recv_h[pl.ds(8 * i, 8)].reshape(768, 128).astype(F32)
        low = jnp.concatenate(ids, axis=1) % 512
        pick = zero_one(iota((512, 768), 0) == low)
        column = jnp.concatenate(
            [jnp.broadcast_to((r // 512).astype(F32), (128, 128)).T for r in ids], axis=0
        )
        for k in range(0, 4, 2):
            both = [jnp.where(column == float(k + n), values, 0.0).astype(BF16) for n in range(2)]
            part = dot(pick, jnp.concatenate(both, axis=1))
            hot[k * 512 : (k + 1) * 512, :] += part[:, 0:128]
            hot[(k + 1) * 512 : (k + 2) * 512, :] += part[:, 128:256]
        return carry

    def hot_group(i):
        some = recv_h.at[8 * i : 8 * i + 8]
        pltpu.make_async_copy(some, some, a_r.at[2 + i]).wait()
        hot_part(i, 0)

    hot_group(0)
    hot_group(1)

    for way in range(2):
        f_copy(way).wait()

        def way_add(j, carry):
            total = fx[next_x[way], 8 * way + j].astype(F32) + fx_recv[way, j].astype(F32)
            fx_sum[way, j] = total.astype(BF16)
            return carry

        lax.fori_loop(0, 8, way_add, 0)
        f_copy(4 + way).start()

    hot_group(2)

    def halves(total, count, width):
        top, bottom = total[0:count], total[count : 2 * count]
        left_half = iota((count, 128), 1) % (2 * width) < width
        return (
            jnp.where(left_half, top, pltpu.roll(bottom, width, 1)),
            jnp.where(left_half, pltpu.roll(top, 128 - width, 1), bottom),
        )

    def z_copy(buf, into, send_sem, recv_sem, d):
        to, device = along_z(d)
        return remote(buf.at[to], into.at[d - 1], send_sem.at[d - 1], recv_sem.at[d - 1], device)

    for n in range(2, 6):
        f_copy(n).wait()
    for y in range(4):
        for z in range(4):
            at = 4 * y + z
            way = at // 8
            total = fx[xx, at].astype(F32) + fx_recv[3 - way, at % 8].astype(F32) + fx_recv[4 + way, at % 8].astype(F32)
            for k, half in enumerate(halves(total, 16, 32)):
                fz[8 * y + 4 * k + z] = half.astype(BF16)
    here = yy * 8 + deep

    def fz_to(d, carry):
        to = lax.rem(here + d, 32)
        z = lax.rem(to, 8)
        device = ((z // 4) * 4 + xx, shard_at(to // 8, lax.rem(z, 4), core))
        remote(fz.at[to], fz_recv.at[d], fz_s.at[0], fz_r.at[0], device).start()
        return carry

    lax.fori_loop(1, 32, fz_to, 0)

    for d in range(1, 4):
        y_copy(wy, wy_recv, wy_s, wy_r, d).wait()

    for j in range(4):
        total = wy[4 * yy + j].astype(F32)
        for d in range(3):
            total = total + wy_recv[d, j].astype(F32)
        for k, half in enumerate(halves(total, 56, 64)):
            wz[4 * k + j] = jnp.concatenate([half, jnp.zeros((8, 128), F32)], axis=0).astype(BF16)
    for d in range(1, 8):
        z_copy(wz, wz_recv, wz_s, wz_r, d).start()

    hot_group(3)
    save_hot = pltpu.make_async_copy(hot, hot_hbm, load_s.at[6])
    save_hot.start()

    for d in range(1, GROUPS):
        mid_copy(d).wait()
    total = mid_send[xx * 2 + zh].astype(F32)
    for d in range(GROUPS - 1):
        total = total + mid_recv[d].astype(F32)
    mout_ref[...] = total

    for d in range(1, 8):
        z_copy(wz, wz_recv, wz_s, wz_r, d).wait()
    total = wz[deep].astype(F32)
    for d in range(7):
        total = total + wz_recv[d].astype(F32)
    wout_ref[0:56, :] = total[0:56]
    wout_ref[56:PAD_W, :] = pltpu.roll(total, 64, 1)[0:56]
    wout_ref[PAD_W:128, :] = jnp.zeros((128 - PAD_W, 128), F32)

    arrived = fz_recv.at[1:32]
    pltpu.make_async_copy(arrived, arrived, fz_r.at[0]).wait()
    total = fz[here].astype(F32)
    for d in range(1, 32):
        total = total + fz_recv[d].astype(F32)
    fout_ref[0:16, :] = total[:, 0:32]
    fout_ref[16:32, :] = pltpu.roll(total, 96, 1)[:, 0:32]
    lout_ref[0:16, :] = pltpu.roll(total, 64, 1)[:, 0:32]
    lout_ref[16:32, :] = pltpu.roll(total, 32, 1)[:, 0:32]

    pltpu.make_async_copy(arrived, arrived, fz_s.at[0]).wait()
    save_hot.wait()
    sent = send_c.at[pl.ds(1, SHARDS - 1)]
    pltpu.make_async_copy(sent, sent, a_s.at[0]).wait()
    sent = recv_m.at[pl.ds(1, SHARDS - 1)]
    pltpu.make_async_copy(sent, sent, a_s.at[1]).wait()
    sent = send_h.at[pl.ds(1, SHARDS - 1)]
    pltpu.make_async_copy(sent, sent, a_s.at[2]).wait()


def finish(dense, hot, weight, first, last, mid, dense_out, hot_out, weight_out, first_out, last_out, mid_out):
    dense_out[...] = dense[...]
    hot_out[...] = hot[...]
    weight_out[...] = weight[...].T[0:64, 0:BLOCK_W]
    first_out[...] = first[...]
    last_out[...] = last[...]
    for m1 in range(8):
        parts = []
        for a in range(4):
            for e2 in range(2):
                row = a * 8 + e2 * 4
                parts.append(mid[row : row + 4, m1 * 32 : (m1 + 1) * 32])
        rows = jnp.concatenate(parts, axis=1)
        for m0 in range(4):
            mid_out[m0 * 8 + m1 : m0 * 8 + m1 + 1, :] = rows[m0 : m0 + 1, :]


def body(
    top_input,
    pre_act,
    grad_hidden,
    top_weight,
    core_first,
    core_mid,
    core_last,
    bag_ids,
    lookup_order,
    hot_rows,
    cold_digits,
):
    vmem = pl.BlockSpec(memory_space=pltpu.VMEM)
    smem = pl.BlockSpec(memory_space=pltpu.SMEM)
    hbm = pl.BlockSpec(memory_space=pl.ANY)

    def buf(*shape, dtype=BF16):
        return pltpu.VMEM(shape, dtype)

    dma = pltpu.SemaphoreType.DMA
    shapes = (
        jax.ShapeDtypeStruct((128, 128), BF16),
        jax.ShapeDtypeStruct((2048, 128), F32),
        jax.ShapeDtypeStruct((128, 128), F32),
        jax.ShapeDtypeStruct((32, 32), F32),
        jax.ShapeDtypeStruct((32, 32), F32),
        jax.ShapeDtypeStruct((32, 256), F32),
    )
    outs = pl.pallas_call(
        kernel,
        out_shape=shapes,
        in_specs=[hbm, hbm, hbm, hbm, smem, smem, vmem, vmem, hbm, hbm, hbm],
        out_specs=(vmem, hbm, vmem, vmem, vmem, vmem),
        scratch_shapes=[
            buf(128, 512),
            buf(128, 512),
            buf(3456, 512),
            buf(128, 3456),
            buf(1024, 256),
            buf(1024, 256),
            buf(32, 2048),
            buf(256, 256, dtype=F32),
            buf(256, 256),
            buf(256, 256),
            buf(2048, 128, dtype=F32),
            buf(26 * 128, 128, dtype=F32),
            buf(PER_HOT, 128, dtype=F32),
            buf(SHARDS, 4, 128, dtype=I32),
            buf(SHARDS, PER_COLD, 128),
            buf(SHARDS, PER_HOT, 128),
            buf(SHARDS, PER_COLD, 128),
            buf(SHARDS, PER_HOT, 128),
            buf(SHARDS, 4, 128, dtype=I32),
            buf(2, 16, PAD_W, 128),
            buf(16, PAD_W, 128),
            buf(256, 512),
            buf(4, 16, PAD_W, 128),
            buf(2, 3, 8, PAD_W, 128),
            buf(256, 1024),
            buf(256, 1024),
            buf(2, 1024, 1024),
            buf(8, 256, 128, dtype=F32),
            buf(8, 256, 128, dtype=F32),
            buf(128, 128, dtype=F32),
            buf(256, 1024),
            buf(256, 1024),
            buf(64, 1024, dtype=F32),
            buf(256, 1024),
            buf(256, 1024),
            buf(256, 256, dtype=F32),
            buf(8, 32, 256),
            buf(7, 32, 256),
            buf(2, 4, 16, 32, 128, dtype=F32),
            buf(2, 4, 16, 32, 128),
            buf(4, 16, 32, 128),
            buf(4, 16, 32, 128),
            buf(2, 8, 32, 128),
            buf(6, 8, 32, 128),
            buf(16, PAD_W, 128),
            buf(3, 4, PAD_W, 128),
            buf(8, 64, 128),
            buf(7, 64, 128),
            buf(32, 16, 128),
            buf(32, 16, 128),
            dma((8,)),
            dma((3,)),
            dma((3,)),
            dma((3,)),
            dma((6,)),
            dma((2, 3)),
            dma((2, 3)),
            dma((6,)),
            dma((6,)),
            dma((3,)),
            dma((3,)),
            dma((7,)),
            dma((7,)),
            dma((1,)),
            dma((1,)),
            dma((7,)),
            dma((7,)),
        ],
        compiler_params=pltpu.CompilerParams(
            collective_id=0, has_side_effects=True, vmem_limit_bytes=56 * 1024 * 1024
        ),
    )(
        pre_act,
        grad_hidden,
        top_weight,
        top_input,
        bag_ids,
        lookup_order,
        hot_rows.reshape(24, 128),
        cold_digits.reshape(24, 128),
        core_first,
        core_last,
        core_mid,
    )
    dense_grad, hot_grad, weight_grad, first_grad, last_grad, mid_grad = pl.pallas_call(
        finish,
        out_shape=shapes[:2] + (jax.ShapeDtypeStruct((64, BLOCK_W), F32),) + shapes[3:],
        in_specs=[vmem] * 6,
        out_specs=(vmem,) * 6,
    )(*outs)
    return (hot_grad[None], dense_grad, weight_grad.T, first_grad, mid_grad, last_grad)


def solution(mesh):
    return jax.shard_map(
        body,
        mesh=mesh,
        in_specs=(
            P(("group", "shard"), None),
            P(("group", "shard"), None),
            P(("group", "shard"), None),
            P(),
            P(),
            P(),
            P(),
            P("group", "shard", None),
            P("group", "shard", None),
            P("group", "shard", None),
            P("group", "shard", None, None),
        ),
        out_specs=(
            P("group", "shard", None),
            P(("group", "shard"), None),
            P("shard", "group"),
            P("shard", "group"),
            P("shard", "group"),
            P("shard", "group"),
        ),
        check_vma=False,
    )
```

```python
import functools

import jax
import jax.numpy as jnp
from jax import lax
from jax.experimental import pallas as pl
from jax.experimental.pallas import tpu as pltpu
from jax.sharding import PartitionSpec as P

F32 = jnp.float32
BF16 = jnp.bfloat16
I32 = jnp.int32

E = 128
RANK = 32
E1 = 8
E2 = 2
E3 = 8
HOT_N = 3072
SHARDS = 32
GROUPS = 8
PER_HOT = 96
PER_COLD = 32
BLOCK_W = 108
PAD_W = 112
ROWS = PAD_W + 32
MESH = pl.DeviceIdType.MESH


def iota(shape, dim):
    return lax.broadcasted_iota(I32, shape, dim)


def dot(a, b):
    return jnp.dot(a, b, preferred_element_type=F32)


def dot_nt(a, b):
    return lax.dot_general(a, b, (((1,), (1,)), ((), ())), preferred_element_type=F32)


def zero_one(mask):
    return jnp.where(mask, 1.0, 0.0).astype(BF16)


def kernel(
    act_hbm, hid_hbm, tw_hbm, x_hbm, bags, order, hot_in, dig_in, first_hbm, last_hbm, mid_hbm,
    dense_ref, hot_hbm, wout_ref, fout_ref, lout_ref, mout_ref,
    act_ref, hid_ref, tw_ref, x_ref, first_ref, last_ref, mid_block, mid_turned, midq, midl, hot,
    pooled, stage, meta, send_c, send_h, recv_c, recv_h, recv_m,
    xt, xt_recv, pre2, w_own, ring,
    first_t, last_t, onehot, a_t, c_t, q_t, he, ce, qs, tf, tl, mid_acc, mid_send, mid_recv,
    fl_own, fl_send, fl_recv, fx, fx_sum, fx_recv,
    wy, wy_recv, wz, wz_recv, fz, fz_recv,
    load_s, core_s, core_r, a_s, a_r, ring_s, ring_r, f_s, f_r, wy_s, wy_r, wz_s, wz_r,
    fz_s, fz_r, m_s, m_r,
):
    g = lax.axis_index("group")
    s = lax.axis_index("shard")
    xx = lax.rem(g, 4)
    zh = g // 4
    core = lax.rem(s, 2)
    zl = lax.rem(s // 2, 4)
    yy = s // 8
    deep = zh * 4 + zl

    load_act = pltpu.make_async_copy(act_hbm, act_ref, load_s.at[0])
    load_hid = pltpu.make_async_copy(hid_hbm, hid_ref, load_s.at[1])
    load_x = pltpu.make_async_copy(x_hbm, x_ref, load_s.at[2])
    load_tw = pltpu.make_async_copy(tw_hbm, tw_ref, load_s.at[3])
    load_first = pltpu.make_async_copy(first_hbm, first_ref, load_s.at[4])
    load_last = pltpu.make_async_copy(last_hbm, last_ref, load_s.at[5])
    load_mid = pltpu.make_async_copy(mid_hbm.at[pl.ds(pl.multiple_of(s * 32, 32), 32)], mid_block, load_s.at[7])
    load_act.start()
    load_hid.start()
    load_x.start()
    load_tw.start()
    load_first.start()
    load_last.start()
    load_mid.start()

    def shard_at(y, z, c):
        return y * 8 + z * 2 + c

    def remote(src, dst, send_sem, recv_sem, to):
        return pltpu.make_async_remote_copy(
            src_ref=src, dst_ref=dst, send_sem=send_sem, recv_sem=recv_sem, device_id=to, device_id_type=MESH
        )

    def along_z(d):
        to = lax.rem(deep + d, 8)
        return to, ((to // 4) * 4 + xx, shard_at(yy, lax.rem(to, 4), core))

    partner = (g, shard_at(yy, zl, 1 - core))

    barrier = pltpu.get_barrier_semaphore()

    def greet_shard(k, carry):
        pl.semaphore_signal(barrier, inc=1, device_id=(g, lax.rem(s + k, SHARDS)), device_id_type=MESH)
        return carry

    def greet_group(k, carry):
        pl.semaphore_signal(barrier, inc=1, device_id=(lax.rem(g + k, GROUPS), s), device_id_type=MESH)
        return carry

    def greet_far(k, carry):
        to = lax.rem(yy * 4 + zl + k, 16)
        to = (lax.rem(g + 4, 8), shard_at(to // 4, lax.rem(to, 4), core))
        pl.semaphore_signal(barrier, inc=1, device_id=to, device_id_type=MESH)
        return carry

    lax.fori_loop(1, SHARDS, greet_shard, 0)
    lax.fori_loop(1, GROUPS, greet_group, 0)
    lax.fori_loop(1, 16, greet_far, 0)

    turns = lax.rem(s, 4)

    def turned(values, width):
        out = values
        for n in range(1, 4):
            out = jnp.where(turns == n, pltpu.roll(values, (4 - n) * width, 1), out)
        return out

    def kept(values, width, i):
        low = lax.rem(i + 4 - turns, 4) * width
        lane = iota(values.shape, 1)
        return jnp.where((lane >= low) & (lane < low + width), values, 0)

    hots = turned(jnp.concatenate([hot_in[pl.ds(c, 8, stride=3), :] for c in range(3)], axis=1), PER_HOT)
    one_three = turned(dig_in[0:8, :] + dig_in[16:24, :] * 65536, PER_COLD)
    two = turned(dig_in[8:16, :] % 32 * 65536, PER_COLD)
    for i in range(4):
        hot_i = kept(hots, PER_HOT, i)
        rows = [hot_i[:, c * 128 : (c + 1) * 128] for c in range(3)] + [kept(one_three, PER_COLD, i)]
        rows[0] = rows[0] + kept(two, PER_COLD, i)
        for q in range(8):
            for c in range(4):
                meta[4 * q + i, c : c + 1, :] = rows[c][q : q + 1, :]

    load_act.wait()
    load_hid.wait()
    pre = jnp.where(act_ref[...].astype(F32) > 0, hid_ref[...].astype(F32), 0.0).astype(BF16)
    col = iota((512, 512), 1)
    source = (col // 64 % 2) * 256 + (col // 128) * 64 + col % 64
    pre2[0:128, :] = dot(pre, zero_one(iota((512, 512), 0) == source)).astype(BF16)

    load_x.wait()
    for shard in range(SHARDS):
        lo = shard * BLOCK_W // 128 * 128
        off = shard * BLOCK_W - lo
        width = 128 if off + BLOCK_W <= 128 else 256
        pick = zero_one(iota((PAD_W, width), 1) == iota((PAD_W, width), 0) + off)
        xt[shard % 2, shard // 2] = dot_nt(pick, x_ref[:, lo : lo + width]).astype(BF16)

    load_tw.wait()
    dense_ref[...] = dot_nt(pre, tw_ref[0:128, :]).astype(BF16)
    for i in range(13):
        part = dot_nt(pre, tw_ref[128 + i * 256 : 384 + i * 256, :]).astype(BF16).astype(F32)
        pooled[pl.ds(2 * i, 128, stride=26), :] = part[:, 0:128]
        pooled[pl.ds(2 * i + 1, 128, stride=26), :] = part[:, 128:256]

    def gather(base, count):
        for j in range(count):
            r = bags[0, 0, order[0, 0, base + j]]
            stage[pl.ds(j, 1), :] = pooled[pl.ds(r, 1), :]
        return stage[0:count, :].astype(BF16)

    def cold_for(k, carry):
        o = lax.rem(s + k, SHARDS)
        send_c[k] = gather(HOT_N + o * PER_COLD, PER_COLD)
        return carry

    lax.fori_loop(0, SHARDS, cold_for, 0)

    def hot_for(k, carry):
        o = lax.rem(s + k, SHARDS)
        send_h[k] = gather(o * PER_HOT, PER_HOT)
        return carry

    lax.fori_loop(0, SHARDS, hot_for, 0)

    pl.semaphore_wait(barrier, SHARDS - 1 + GROUPS - 1 + 15)
    send_pre = remote(pre2.at[0:128], pre2.at[128:256], core_s.at[0], core_r.at[0], partner)
    send_pre.start()
    send_xt = remote(xt.at[1 - core], xt_recv, core_s.at[1], core_r.at[1], partner)
    send_xt.start()

    def cold_to(k, carry):
        o = lax.rem(s + k, SHARDS)
        remote(send_c.at[k], recv_c.at[k], a_s.at[0], a_r.at[0], (g, o)).start()
        remote(meta.at[o], recv_m.at[k], a_s.at[1], a_r.at[1], (g, o)).start()
        return carry

    lax.fori_loop(1, SHARDS, cold_to, 0)
    pltpu.make_async_copy(send_c.at[0], recv_c.at[0], a_r.at[0]).start()
    pltpu.make_async_copy(meta.at[s], recv_m.at[0], a_r.at[1]).start()

    send_pre.wait()
    send_xt.wait()
    pre_both = pre2[...]
    for j in range(0, 16, 4):
        both = jnp.concatenate(
            [xt[core, j : j + 4].reshape(4 * PAD_W, 128), xt_recv[j : j + 4].reshape(4 * PAD_W, 128)], axis=1
        )
        part = dot(both, pre_both).astype(BF16)
        for k in range(4):
            w_own[k, j : j + 4] = part[:, k * 128 : (k + 1) * 128].reshape(4, PAD_W, 128)

    right = (zh * 4 + lax.rem(xx + 1, 4), s)
    left = (zh * 4 + lax.rem(xx + 3, 4), s)

    def ring_copy(way, step):
        to = right if way == 0 else left
        if step == 0:
            chunk = lax.rem(xx + 3, 4) if way == 0 else lax.rem(xx + 1, 4)
            src = w_own.at[chunk, pl.ds(way * 8, 8)]
        else:
            src = ring.at[way, step - 1]
        return remote(src, ring.at[way, step], ring_s.at[way, step], ring_r.at[way, step], to)

    def ring_add(way, step):
        chunk = lax.rem(xx + 2 - step, 4) if way == 0 else lax.rem(xx + 2 + step, 4)

        def add(j, carry):
            total = ring[way, step, j].astype(F32) + w_own[chunk, way * 8 + j].astype(F32)
            ring[way, step, j] = total.astype(BF16)
            return carry

        lax.fori_loop(0, 8, add, 0, unroll=4)

    def ring_next(step):
        for way in range(2):
            ring_copy(way, step - 1).wait()
            ring_add(way, step - 1)
            ring_copy(way, step).start()

    for way in range(2):
        ring_copy(way, 0).start()

    def hot_to(k, carry):
        o = lax.rem(s + k, SHARDS)
        remote(send_h.at[k], recv_h.at[k], a_s.at[2], a_r.at[2 + k // 8], (g, o)).start()
        return carry

    lax.fori_loop(1, 4, hot_to, 0)
    pltpu.make_async_copy(send_h.at[0], recv_h.at[0], a_r.at[2]).start()

    load_first.wait()
    load_last.wait()
    eye = zero_one(iota((256, 256), 0) == iota((256, 256), 1))
    first_t[...] = dot_nt(eye, first_ref[...]).astype(BF16)
    turn_row = iota((256, 256), 0)
    turn = zero_one(iota((256, 256), 1) == (turn_row % 32) * 8 + turn_row // 32)
    last_t[...] = dot_nt(turn, last_ref[...]).astype(BF16)
    load_mid.wait()
    block = mid_block[...].astype(F32)
    sub = iota((8, 128), 0) % 4
    apart = (sub + 4 - iota((8, 128), 1) // 32) % 4
    for m0 in range(4):
        for c in range(16):
            value = block[m0 * 8 : (m0 + 1) * 8, c * 128 : (c + 1) * 128]
            out = value
            for d in range(1, 4):
                moved = pltpu.roll(value, 128 - 32 * d, 1)
                moved = jnp.where(sub >= d, pltpu.roll(moved, d, 0), pltpu.roll(moved, d + 4, 0))
                out = jnp.where(apart == d, moved, out)
            row = m0 * 64 + c * 4
            mid_turned[row : row + 4, 0:128] = out[0:4]
            mid_turned[row : row + 4, 128:256] = out[4:8]
    source = turn_row // 64 * 64 + turn_row % 32 * 2 + turn_row // 32 % 2
    midq[...] = dot(zero_one(iota((256, 256), 1) == source), mid_turned[...].astype(BF16)).astype(BF16)
    midl[...] = dot_nt(eye, midq[...]).astype(BF16)
    mid_acc[...] = jnp.zeros_like(mid_acc)

    pltpu.make_async_copy(recv_c, recv_c, a_r.at[0]).wait()
    pltpu.make_async_copy(recv_m, recv_m, a_r.at[1]).wait()

    def words(t, row):
        four = recv_m[pl.ds(4 * t, 4), row : row + 1, :]
        return four[0] + four[1] + four[2] + four[3]

    def pick_cores(u, carry):
        lanes = pl.ds(pl.multiple_of(u * 256, 256), 256)
        both = jnp.concatenate([words(2 * u, 3), words(2 * u + 1, 3)], axis=1)
        for i, (table, out) in enumerate(((first_t, a_t), (last_t, c_t))):
            digit = both % 65536 if i == 0 else both // 65536
            for k in range(4):
                row = iota((256, 256), 0) + k * 256
                onehot[i, k * 256 : (k + 1) * 256, lanes] = zero_one(row == digit)
            part = dot(table[...], onehot[i, :, lanes])
            out[2 * u] = part[:, 0:128]
            out[2 * u + 1] = part[:, 128:256]
        return carry

    lax.fori_loop(0, 4, pick_cores, 0, unroll=2)

    def cold_tile(t, carry):
        lax.fori_loop(4 * t + 4, jnp.minimum(4 * t + 8, SHARDS), hot_to, 0)
        lanes = pl.ds(pl.multiple_of(t * 128, 128), 128)
        two = words(t, 0) // 65536
        q_t[...] = recv_c[pl.ds(4 * t, 4)].reshape(128, 128).astype(F32).T
        low = jnp.broadcast_to(jnp.concatenate([two // 8, two // 8], axis=1), (8, 256))
        high = jnp.broadcast_to(jnp.concatenate([two % 8, two % 8], axis=1), (8, 256))
        is_low = [low == k for k in range(4)]
        is_high = [high == k for k in range(8)]

        def packed(mask):
            half = jnp.where(mask, 1.0, 0.0)
            return jnp.concatenate([half, half], axis=0).astype(BF16)

        keep_low = [packed(m) for m in is_low]
        keep_high = [packed(m) for m in is_high]
        for pair in range(4):
            cols = slice(pair * 256, (pair + 1) * 256)
            for e2 in range(2):
                halves = []
                for e3 in (2 * pair, 2 * pair + 1):
                    total = None
                    for e1 in range(8):
                        q_row = e1 * 16 + e2 * 8 + e3
                        term = a_t[t, e1 * 32 : (e1 + 1) * 32, :] * q_t[q_row : q_row + 1, :]
                        total = term if total is None else total + term
                    halves.append(total)
                h = jnp.concatenate(halves, axis=1).astype(BF16).reshape(2, 16, 256)
                for k in range(4):
                    he[k * 64 + e2 * 32 : k * 64 + e2 * 32 + 32, cols] = (h * keep_low[k][None]).reshape(32, 256)
            c = jnp.concatenate(
                [c_t[t, e3 * 32 : (e3 + 1) * 32, :] for e3 in (2 * pair, 2 * pair + 1)], axis=1
            )
            c = c.astype(BF16).reshape(2, 16, 256)
            for k in range(8):
                ce[k * 32 : (k + 1) * 32, cols] = (c * keep_high[k][None]).reshape(32, 256)
            q_all = dot(midq[...], ce[:, cols]).reshape(4, 8, 8, 256)
            total = q_all[0]
            for k in range(1, 4):
                total = jnp.where(is_low[k][None], q_all[k], total)
            qs[:, cols] = total.reshape(64, 256)
            l_all = dot(midl[...], he[:, cols]).reshape(8, 4, 8, 256)
            total = l_all[0]
            for k in range(1, 8):
                total = jnp.where(is_high[k][None], l_all[k], total)
            total = total.reshape(32, 256).astype(BF16)
            tl[pair * 64 : pair * 64 + 32, lanes] = total[:, 0:128]
            tl[pair * 64 + 32 : pair * 64 + 64, lanes] = total[:, 128:256]
        mid_acc[...] += dot_nt(he[...], ce[...])
        for e1 in range(8):
            total = None
            for e2 in range(2):
                for e3 in range(8):
                    q_row = e1 * 16 + e2 * 8 + e3
                    term = qs[e2 * 32 : (e2 + 1) * 32, e3 * 128 : (e3 + 1) * 128] * q_t[q_row : q_row + 1, :]
                    total = term if total is None else total + term
            row = (e1 % 4) * 64 + (e1 // 4) * 32
            tf[row : row + 32, lanes] = total.astype(BF16)
        return carry

    ring_next(1)
    lax.fori_loop(0, 6, cold_tile, 0)
    ring_next(2)
    lax.fori_loop(6, 8, cold_tile, 0)

    row = iota((256, 256), 0)
    j = row % 32
    source = (j % 8) * 32 + ((row // 32 % 2) * 4 + row // 64) * 4 + j // 8
    tl[...] = dot(zero_one(iota((256, 256), 1) == source), tl[...]).astype(BF16)
    lane = iota((256, 128), 1)

    def by_digit(k, carry):
        rows = pl.ds(pl.multiple_of(k * 256, 256), 256)
        one = dot_nt(onehot[0, rows, :], tf[...])
        two = dot_nt(onehot[1, rows, :], tl[...])
        for i in range(4):
            a = one[:, i // 2 * 128 : i // 2 * 128 + 128]
            b = two[:, i // 2 * 128 : i // 2 * 128 + 128]
            if i % 2 == 0:
                part = jnp.where(lane < 64, a, pltpu.roll(b, 64, 1))
            else:
                part = jnp.where(lane < 64, pltpu.roll(a, 64, 1), b)
            for n in range(8):
                block = part[n * 32 : (n + 1) * 32, :]
                fl_own[n % 2, i, 4 * k + n // 2] = block
                fl_send[n % 2, i, 4 * k + n // 2] = block.astype(BF16)
        return carry

    lax.fori_loop(0, 4, by_digit, 0, unroll=2)

    fl_copy = remote(fl_send.at[1 - core], fl_recv, core_s.at[2], core_r.at[2], partner)
    fl_copy.start()

    row = iota((256, 256), 0)
    source = (row % 4) * 64 + (row // 4 % 2) * 32 + ((row // 32 % 2) * 4 + row // 64) * 4 + row // 8 % 4
    moved = dot(zero_one(iota((256, 256), 1) == source), mid_acc[...].astype(BF16)).astype(BF16)
    for k in range(8):
        mid_send[k] = moved[k * 32 : (k + 1) * 32, :]

    def mid_copy(d):
        to = lax.rem(g + d, GROUPS)
        src = mid_send.at[lax.rem(to, 4) * 2 + to // 4]
        return remote(src, mid_recv.at[d - 1], m_s.at[d - 1], m_r.at[d - 1], (to, s))

    for d in range(1, GROUPS):
        mid_copy(d).start()

    for way in range(2):
        ring_copy(way, 2).wait()

        def last_add(j, carry):
            total = ring[way, 2, j].astype(F32) + w_own[xx, way * 8 + j].astype(F32)
            wy[way * 8 + j] = total.astype(BF16)
            return carry

        lax.fori_loop(0, 8, last_add, 0, unroll=4)

    def y_copy(buf, into, send_sem, recv_sem, d):
        to = lax.rem(yy + d, 4)
        src = buf.at[pl.ds(4 * to, 4)]
        return remote(src, into.at[d - 1], send_sem.at[d - 1], recv_sem.at[d - 1], (g, shard_at(to, zl, core)))

    for d in range(1, 4):
        y_copy(wy, wy_recv, wy_s, wy_r, d).start()

    fl_copy.wait()

    def fl_pair(j, carry):
        for k in range(4):
            fx[k, j] = (fl_own[core, k, j] + fl_recv[k, j].astype(F32)).astype(BF16)
        return carry

    lax.fori_loop(0, 16, fl_pair, 0, unroll=4)
    next_x = (lax.rem(xx + 1, 4), lax.rem(xx + 3, 4))
    far_x = lax.rem(xx + 2, 4)
    low_half, high_half = pl.ds(0, 8), pl.ds(8, 8)

    def f_copy(n):
        way = n % 2
        half = (low_half, high_half)[way]
        rest = (high_half, low_half)[way]
        src = (fx.at[far_x, half], fx.at[next_x[way], rest], fx_sum.at[way])[n // 2]
        return remote(src, fx_recv.at[n], f_s.at[n], f_r.at[n], (right, left)[way])

    for n in range(4):
        f_copy(n).start()

    hot[...] = jnp.zeros_like(hot)

    def hot_part(i, carry):
        ids = []
        for half in range(2):
            four = recv_m[pl.ds(8 * i + 4 * half, 4), :, :]
            four = four[0] + four[1] + four[2] + four[3]
            ids += [four[k : k + 1, :] % 65536 for k in range(3)]
        values = recv_h[pl.ds(8 * i, 8)].reshape(768, 128).astype(F32)
        low = jnp.concatenate(ids, axis=1) % 512
        pick = zero_one(iota((512, 768), 0) == low)
        column = jnp.concatenate(
            [jnp.broadcast_to((r // 512).astype(F32), (128, 128)).T for r in ids], axis=0
        )
        for k in range(0, 4, 2):
            both = [jnp.where(column == float(k + n), values, 0.0).astype(BF16) for n in range(2)]
            part = dot(pick, jnp.concatenate(both, axis=1))
            hot[k * 512 : (k + 1) * 512, :] += part[:, 0:128]
            hot[(k + 1) * 512 : (k + 2) * 512, :] += part[:, 128:256]
        return carry

    def hot_group(i):
        some = recv_h.at[8 * i : 8 * i + 8]
        pltpu.make_async_copy(some, some, a_r.at[2 + i]).wait()
        hot_part(i, 0)

    hot_group(0)
    hot_group(1)

    for way in range(2):
        f_copy(way).wait()

        def way_add(j, carry):
            total = fx[next_x[way], 8 * way + j].astype(F32) + fx_recv[way, j].astype(F32)
            fx_sum[way, j] = total.astype(BF16)
            return carry

        lax.fori_loop(0, 8, way_add, 0, unroll=4)
        f_copy(4 + way).start()

    hot_group(2)

    def halves(total, count, width):
        top, bottom = total[0:count], total[count : 2 * count]
        left_half = iota((count, 128), 1) % (2 * width) < width
        return (
            jnp.where(left_half, top, pltpu.roll(bottom, width, 1)),
            jnp.where(left_half, pltpu.roll(top, 128 - width, 1), bottom),
        )

    def z_copy(buf, into, send_sem, recv_sem, d):
        to, device = along_z(d)
        return remote(buf.at[to], into.at[d - 1], send_sem.at[d - 1], recv_sem.at[d - 1], device)

    for n in range(2, 6):
        f_copy(n).wait()
    for y in range(4):
        for z in range(4):
            at = 4 * y + z
            way = at // 8
            total = fx[xx, at].astype(F32) + fx_recv[3 - way, at % 8].astype(F32) + fx_recv[4 + way, at % 8].astype(F32)
            for k, half in enumerate(halves(total, 16, 32)):
                fz[8 * y + 4 * k + z] = half.astype(BF16)
    here = yy * 8 + deep

    def fz_to(d, carry):
        to = lax.rem(here + d, 32)
        z = lax.rem(to, 8)
        device = ((z // 4) * 4 + xx, shard_at(to // 8, lax.rem(z, 4), core))
        remote(fz.at[to], fz_recv.at[d], fz_s.at[0], fz_r.at[0], device).start()
        return carry

    lax.fori_loop(1, 32, fz_to, 0)

    for d in range(1, 4):
        y_copy(wy, wy_recv, wy_s, wy_r, d).wait()

    for j in range(4):
        total = wy[4 * yy + j].astype(F32)
        for d in range(3):
            total = total + wy_recv[d, j].astype(F32)
        for k, half in enumerate(halves(total, 56, 64)):
            wz[4 * k + j] = jnp.concatenate([half, jnp.zeros((8, 128), F32)], axis=0).astype(BF16)
    for d in range(1, 8):
        z_copy(wz, wz_recv, wz_s, wz_r, d).start()

    hot_group(3)
    save_hot = pltpu.make_async_copy(hot, hot_hbm, load_s.at[6])
    save_hot.start()

    for d in range(1, GROUPS):
        mid_copy(d).wait()
    total = mid_send[xx * 2 + zh].astype(F32)
    for d in range(GROUPS - 1):
        total = total + mid_recv[d].astype(F32)
    mout_ref[...] = total

    for d in range(1, 8):
        z_copy(wz, wz_recv, wz_s, wz_r, d).wait()
    total = wz[deep].astype(F32)
    for d in range(7):
        total = total + wz_recv[d].astype(F32)
    wout_ref[0:56, :] = total[0:56]
    wout_ref[56:PAD_W, :] = pltpu.roll(total, 64, 1)[0:56]
    wout_ref[PAD_W:128, :] = jnp.zeros((128 - PAD_W, 128), F32)

    arrived = fz_recv.at[1:32]
    pltpu.make_async_copy(arrived, arrived, fz_r.at[0]).wait()
    total = fz[here].astype(F32)
    for d in range(1, 32):
        total = total + fz_recv[d].astype(F32)
    fout_ref[0:16, :] = total[:, 0:32]
    fout_ref[16:32, :] = pltpu.roll(total, 96, 1)[:, 0:32]
    lout_ref[0:16, :] = pltpu.roll(total, 64, 1)[:, 0:32]
    lout_ref[16:32, :] = pltpu.roll(total, 32, 1)[:, 0:32]

    pltpu.make_async_copy(arrived, arrived, fz_s.at[0]).wait()
    save_hot.wait()
    sent = send_c.at[pl.ds(1, SHARDS - 1)]
    pltpu.make_async_copy(sent, sent, a_s.at[0]).wait()
    sent = recv_m.at[pl.ds(1, SHARDS - 1)]
    pltpu.make_async_copy(sent, sent, a_s.at[1]).wait()
    sent = send_h.at[pl.ds(1, SHARDS - 1)]
    pltpu.make_async_copy(sent, sent, a_s.at[2]).wait()


def finish(dense, hot, weight, first, last, mid, dense_out, hot_out, weight_out, first_out, last_out, mid_out):
    dense_out[...] = dense[...]
    hot_out[...] = hot[...]
    weight_out[...] = weight[...].T[0:64, 0:BLOCK_W]
    first_out[...] = first[...]
    last_out[...] = last[...]
    for m1 in range(8):
        parts = []
        for a in range(4):
            for e2 in range(2):
                row = a * 8 + e2 * 4
                parts.append(mid[row : row + 4, m1 * 32 : (m1 + 1) * 32])
        rows = jnp.concatenate(parts, axis=1)
        for m0 in range(4):
            mid_out[m0 * 8 + m1 : m0 * 8 + m1 + 1, :] = rows[m0 : m0 + 1, :]


def body(
    top_input,
    pre_act,
    grad_hidden,
    top_weight,
    core_first,
    core_mid,
    core_last,
    bag_ids,
    lookup_order,
    hot_rows,
    cold_digits,
):
    vmem = pl.BlockSpec(memory_space=pltpu.VMEM)
    smem = pl.BlockSpec(memory_space=pltpu.SMEM)
    hbm = pl.BlockSpec(memory_space=pl.ANY)

    def buf(*shape, dtype=BF16):
        return pltpu.VMEM(shape, dtype)

    dma = pltpu.SemaphoreType.DMA
    shapes = (
        jax.ShapeDtypeStruct((128, 128), BF16),
        jax.ShapeDtypeStruct((2048, 128), F32),
        jax.ShapeDtypeStruct((128, 128), F32),
        jax.ShapeDtypeStruct((32, 32), F32),
        jax.ShapeDtypeStruct((32, 32), F32),
        jax.ShapeDtypeStruct((32, 256), F32),
    )
    outs = pl.pallas_call(
        kernel,
        out_shape=shapes,
        in_specs=[hbm, hbm, hbm, hbm, smem, smem, vmem, vmem, hbm, hbm, hbm],
        out_specs=(vmem, hbm, vmem, vmem, vmem, vmem),
        scratch_shapes=[
            buf(128, 512),
            buf(128, 512),
            buf(3456, 512),
            buf(128, 3456),
            buf(1024, 256),
            buf(1024, 256),
            buf(32, 2048),
            buf(256, 256, dtype=F32),
            buf(256, 256),
            buf(256, 256),
            buf(2048, 128, dtype=F32),
            buf(26 * 128, 128, dtype=F32),
            buf(PER_HOT, 128, dtype=F32),
            buf(SHARDS, 4, 128, dtype=I32),
            buf(SHARDS, PER_COLD, 128),
            buf(SHARDS, PER_HOT, 128),
            buf(SHARDS, PER_COLD, 128),
            buf(SHARDS, PER_HOT, 128),
            buf(SHARDS, 4, 128, dtype=I32),
            buf(2, 16, PAD_W, 128),
            buf(16, PAD_W, 128),
            buf(256, 512),
            buf(4, 16, PAD_W, 128),
            buf(2, 3, 8, PAD_W, 128),
            buf(256, 1024),
            buf(256, 1024),
            buf(2, 1024, 1024),
            buf(8, 256, 128, dtype=F32),
            buf(8, 256, 128, dtype=F32),
            buf(128, 128, dtype=F32),
            buf(256, 1024),
            buf(256, 1024),
            buf(64, 1024, dtype=F32),
            buf(256, 1024),
            buf(256, 1024),
            buf(256, 256, dtype=F32),
            buf(8, 32, 256),
            buf(7, 32, 256),
            buf(2, 4, 16, 32, 128, dtype=F32),
            buf(2, 4, 16, 32, 128),
            buf(4, 16, 32, 128),
            buf(4, 16, 32, 128),
            buf(2, 8, 32, 128),
            buf(6, 8, 32, 128),
            buf(16, PAD_W, 128),
            buf(3, 4, PAD_W, 128),
            buf(8, 64, 128),
            buf(7, 64, 128),
            buf(32, 16, 128),
            buf(32, 16, 128),
            dma((8,)),
            dma((3,)),
            dma((3,)),
            dma((3,)),
            dma((6,)),
            dma((2, 3)),
            dma((2, 3)),
            dma((6,)),
            dma((6,)),
            dma((3,)),
            dma((3,)),
            dma((7,)),
            dma((7,)),
            dma((1,)),
            dma((1,)),
            dma((7,)),
            dma((7,)),
        ],
        compiler_params=pltpu.CompilerParams(
            collective_id=0, has_side_effects=True, vmem_limit_bytes=56 * 1024 * 1024
        ),
    )(
        pre_act,
        grad_hidden,
        top_weight,
        top_input,
        bag_ids,
        lookup_order,
        hot_rows.reshape(24, 128),
        cold_digits.reshape(24, 128),
        core_first,
        core_last,
        core_mid,
    )
    dense_grad, hot_grad, weight_grad, first_grad, last_grad, mid_grad = pl.pallas_call(
        finish,
        out_shape=shapes[:2] + (jax.ShapeDtypeStruct((64, BLOCK_W), F32),) + shapes[3:],
        in_specs=[vmem] * 6,
        out_specs=(vmem,) * 6,
    )(*outs)
    return (hot_grad[None], dense_grad, weight_grad.T, first_grad, mid_grad, last_grad)


def solution(mesh):
    return jax.shard_map(
        body,
        mesh=mesh,
        in_specs=(
            P(("group", "shard"), None),
            P(("group", "shard"), None),
            P(("group", "shard"), None),
            P(),
            P(),
            P(),
            P(),
            P("group", "shard", None),
            P("group", "shard", None),
            P("group", "shard", None),
            P("group", "shard", None, None),
        ),
        out_specs=(
            P("group", "shard", None),
            P(("group", "shard"), None),
            P("shard", "group"),
            P("shard", "group"),
            P("shard", "group"),
            P("shard", "group"),
        ),
        check_vma=False,
    )
```
